32 devices in a mesh: scalar: 4 (over z), space: 8 (over y, x, core).
Axes of the slice: x: 2, y: 2, z: 4, core: 2. Of those that a mesh axis runs over, the one named last changes fastest.
Arguments:
- scalars: float32 [16, 2, 1024, 1024], P('scalar', None, 'space'), may hold values from -6 to 6
- velocity_x: float32 [2, 1024, 1024], P(None, 'space', 'scalar'), may hold values from 0 to 1, as said below
- velocity_y: float32 [2, 1024, 1024], P(None, 'space', 'scalar'), may hold values from 0 to 1, as said below
- shift_x: int32 [2, 1024], P(None, 'space'), may hold values from -8 to 8
- shift_y: int32 [1024], P('space'), may hold values from -8 to 8
- schmidt: int32 [16], P('scalar'), may hold values from 1 to 5
Outputs:
- transported: float32 [16, 2, 1024, 1024], P('scalar', None, 'space')
The draws below stay inside these ranges and needn't reach their ends.
Inputs may be any that keep to these rules, and one draw needn't show every extreme that they name: shift_x and shift_y are whole cells of displacement along the line; they act periodically. `velocity_x`: fractions of a cell. `velocity_y`: fractions of a cell.
All inputs are finite; a program needn't handle non-finite values.
Results may differ from the reference program's by a relative error of at most 0.0003.
Values sent between devices are 32-bit elements; how exact they have to be, the bound alone decides.
A program may use at most 192 MiB of HBM per device.

```python
import math
import jax
import jax.numpy as jnp
from jax import lax

NSCAL = 16
NX = 1024
NY = 1024
NZ = 2


def draw_scalars(key, part):
    base_key = jax.random.fold_in(key, 101)
    rough_key, angle_key, level_key = jax.random.split(base_key, 3)
    field_shape = (NSCAL, NZ, NY, NX)
    rough_part = jnp.clip(0.5 * jax.random.normal(rough_key, field_shape, jnp.float32), -2.0, 2.0)
    amplitude = 2.5 + 0.0 * jax.random.uniform(level_key, (NSCAL, NZ, 1, 1), jnp.float32)
    angles = jax.random.uniform(angle_key, (NSCAL, NZ, 1, 1), jnp.float32, -math.pi, math.pi)
    row_index = lax.broadcasted_iota(jnp.int32, (1, 1, NY, 1), 2)
    col_index = lax.broadcasted_iota(jnp.int32, (1, 1, 1, NX), 3)
    row_sign = 1.0 - 2.0 * (row_index % 2).astype(jnp.float32)
    col_sign = 1.0 - 2.0 * (col_index % 2).astype(jnp.float32)
    result = rough_part + amplitude * jnp.cos(angles) * col_sign + amplitude * jnp.sin(angles) * row_sign
    return result.astype(jnp.float32)


def fraction_draw(key, salt):
    base_key = jax.random.fold_in(key, salt)
    field_shape = (NZ, NY, NX)
    values = jax.random.uniform(base_key, field_shape, jnp.float32, 0.0, 0.2)
    return values.astype(jnp.float32)


def draw_velocity_x(key, part):
    return fraction_draw(key, 211)


def draw_velocity_y(key, part):
    return fraction_draw(key, 307)


def set_ends(values, own_key, smallest, largest):
    spot = [jax.random.randint(jax.random.fold_in(own_key, axis), (), 0, length) for axis, length in enumerate(values.shape)]
    longest = values.shape.index(max(values.shape))
    beside = spot[:longest] + [(spot[longest] + 1) % values.shape[longest]] + spot[longest + 1:]
    return values.at[tuple(spot)].set(smallest).at[tuple(beside)].set(largest)


def setup_inputs(seed: int = 0) -> dict:
    splits = jax.random.split(jax.random.key(seed), 7)
    scalars = draw_scalars(jax.random.fold_in(splits[6], 71), 0)
    velocity_x = draw_velocity_x(jax.random.fold_in(splits[6], 71), 0)
    velocity_y = draw_velocity_y(jax.random.fold_in(splits[6], 71), 0)
    shift_x = set_ends(jax.random.randint(splits[3], (NZ, NY), -8, 9), jax.random.fold_in(splits[3], 1), -8, 8).astype(jnp.int32)
    shift_y = set_ends(jax.random.randint(splits[4], (NX,), -8, 9), jax.random.fold_in(splits[4], 1), -8, 8).astype(jnp.int32)
    schmidt = set_ends(jax.random.randint(splits[5], (NSCAL,), 1, 6), jax.random.fold_in(splits[5], 1), 1, 5).astype(jnp.int32)
    return {"scalars": scalars, "velocity_x": velocity_x, "velocity_y": velocity_y, "shift_x": shift_x, "shift_y": shift_y, "schmidt": schmidt}


def spline(distance):
    magnitude = jnp.abs(distance)
    far_part = jnp.maximum(3.0 - magnitude, 0.0)
    middle = jnp.maximum(2.0 - magnitude, 0.0)
    near_part = jnp.maximum(1.0 - magnitude, 0.0)
    return (far_part ** 5 - 6.0 * middle ** 5 + 15.0 * near_part ** 5) / 120.0


def remesh(fields, fraction, shift_line):
    length = fields.shape[-1]
    summed = jnp.zeros_like(fields)
    for offset in range(-2, 4):
        weight = spline(offset - fraction)
        summed = summed + jnp.roll(fields * weight, offset, axis=-1)
    column = lax.broadcasted_iota(jnp.int32, fraction.shape, 2)
    source = (column - shift_line[:, :, None].astype(jnp.int32)) % length
    source = jnp.broadcast_to(source, fields.shape).astype(jnp.int32)
    return jnp.take_along_axis(summed, source, axis=-1)


def diffuse_exact(fields, diffusivity):
    length = fields.shape[-1]
    spectra = jnp.fft.rfft(fields, axis=-1)
    wavenum = jnp.arange(length // 2 + 1).astype(jnp.float32) / (length // 2)
    damping = jnp.exp(-diffusivity * wavenum * wavenum)
    return jnp.fft.irfft(spectra * damping, n=length, axis=-1).astype(jnp.float32)


def reference(scalars, velocity_x, velocity_y, shift_x, shift_y, schmidt):
    inverse_sc = jnp.exp2((3 - schmidt).astype(jnp.float32))
    shift_cols = jnp.broadcast_to(shift_y[None, :], (NZ, NX))
    velocity_turned = jnp.swapaxes(velocity_y, 1, 2)

    def per_scalar(members):
        fields, diffusivity = members
        fields = diffuse_exact(remesh(fields, velocity_x, shift_x), 0.5 * diffusivity)
        turned = jnp.swapaxes(fields, 1, 2)
        turned = diffuse_exact(remesh(turned, velocity_turned, shift_cols), diffusivity)
        fields = jnp.swapaxes(turned, 1, 2)
        return diffuse_exact(remesh(fields, velocity_x, shift_x), 0.5 * diffusivity)

    return lax.map(per_scalar, (scalars, inverse_sc))
```

```python
import functools
import math

import jax
import jax.numpy as jnp
import numpy as np
from jax import lax
from jax.experimental import pallas as pl
from jax.experimental.pallas import tpu as pltpu
from jax.sharding import PartitionSpec as P

NY = 1024


def spline(distance):
    magnitude = jnp.abs(distance)
    far_part = jnp.maximum(3.0 - magnitude, 0.0)
    middle = jnp.maximum(2.0 - magnitude, 0.0)
    near_part = jnp.maximum(1.0 - magnitude, 0.0)
    return (far_part**5 - 6.0 * middle**5 + 15.0 * near_part**5) / 120.0


def remesh(fields, fraction, shift_line):
    summed = jnp.zeros_like(fields)
    for offset in range(-2, 4):
        weight = spline(offset - fraction)
        summed = summed + jnp.roll(fields * weight, offset, axis=-1)
    line_shift = shift_line[None, :, :, None]
    moved = summed
    for amount in range(-8, 9):
        moved = jnp.where(line_shift == amount, jnp.roll(summed, amount, axis=-1), moved)
    return moved


def remesh_columns(fields, fraction, shift_cols):
    summed = jnp.zeros_like(fields)
    for offset in range(-2, 4):
        weight = spline(offset - fraction)
        summed = summed + jnp.roll(fields * weight[None], offset, axis=2)
    column_shift = shift_cols[None, None, None, :]
    moved = summed
    for amount in range(-8, 9):
        moved = jnp.where(column_shift == amount, jnp.roll(summed, amount, axis=2), moved)
    return moved


def spectral_tables(length):
    midpoint = length // 2
    column = jnp.arange(length, dtype=jnp.int32)
    wavenum = jnp.where(column <= midpoint, column, column - midpoint)
    phases = column[:, None] * wavenum[None, :] % length
    angles = phases.astype(jnp.float32) * (2.0 * math.pi / length)
    forward = jnp.where((column <= midpoint)[None, :], jnp.cos(angles), jnp.sin(angles))
    inverse_weight = jnp.where((wavenum == 0) | (column == midpoint), 1.0, 2.0) / length
    inverse = forward.T * inverse_weight[:, None]
    relative = wavenum.astype(jnp.float32) / midpoint
    return (forward, inverse, relative * relative)


def diffuse(fields, diffusivity, tables):
    forward, inverse, wave_square = tables
    initial = fields.shape
    rows_flat = fields.reshape(-1, initial[-1])
    spectra = jnp.dot(
        rows_flat, forward, precision=lax.Precision.HIGHEST, preferred_element_type=jnp.float32
    )
    damping = jnp.exp(-diffusivity[:, None] * wave_square[None, :])
    spectra = spectra.reshape(initial) * damping[:, None, None, :]
    result = jnp.dot(
        spectra.reshape(-1, initial[-1]),
        inverse,
        precision=lax.Precision.HIGHEST,
        preferred_element_type=jnp.float32,
    )
    return result.reshape(initial)


def diffuse_columns(fields, diffusivity, tables):
    forward, inverse, wave_square = tables
    spectra = jnp.einsum(
        "jk,szjx->szkx",
        forward,
        fields,
        precision=lax.Precision.HIGHEST,
        preferred_element_type=jnp.float32,
    )
    damping = jnp.exp(-diffusivity[:, None] * wave_square[None, :])
    spectra = spectra * damping[:, None, :, None]
    return jnp.einsum(
        "kj,szkx->szjx",
        inverse,
        spectra,
        precision=lax.Precision.HIGHEST,
        preferred_element_type=jnp.float32,
    )


def one_sweep(fields, fraction, shift_line, diffusivity, tables):
    return diffuse(remesh(fields, fraction, shift_line), diffusivity, tables)


def fetch_velocity(velocity_x):
    return lax.all_gather(velocity_x, "scalar", axis=2, tiled=True)


def on_device(scalars, velocity_x, velocity_y, shift_x, shift_y, schmidt):
    diffusivity = jnp.exp2((3 - schmidt).astype(jnp.float32))
    tables_x = spectral_tables(scalars.shape[3])
    tables_y = spectral_tables(NY)
    along_x = fetch_velocity(velocity_x)
    fields = one_sweep(scalars, along_x, shift_x, 0.5 * diffusivity, tables_x)
    along_y = lax.all_gather(velocity_y, "scalar", axis=2, tiled=True)
    fields_cols, velocity_cols = (
        lax.all_to_all(fields, "space", split_axis=3, concat_axis=2, tiled=True),
        lax.all_to_all(along_y[None], "space", split_axis=3, concat_axis=2, tiled=True),
    )
    remeshed = remesh_columns(fields_cols, velocity_cols[0], shift_y)
    returned = diffuse_columns(remeshed, diffusivity, tables_y)
    fields = lax.all_to_all(returned, "space", split_axis=2, concat_axis=3, tiled=True)
    along_x = fetch_velocity(velocity_x)
    return one_sweep(fields, along_x, shift_x, 0.5 * diffusivity, tables_x)


BLOCK = 256
REACH = 8
MESH = pl.DeviceIdType.MESH


def spline_weights(f):
    g = 1.0 - f

    def fifth(v):
        w = v * v
        return w * w * v

    f0, f1, f2 = fifth(f), fifth(1.0 + f), fifth(2.0 + f)
    g0, g1, g2 = fifth(g), fifth(1.0 + g), fifth(2.0 + g)
    c = 1.0 / 120.0
    return (
        g0 * c,
        (g1 - 6.0 * g0) * c,
        (g2 - 6.0 * g1 + 15.0 * g0) * c,
        (f2 - 6.0 * f1 + 15.0 * f0) * c,
        (f1 - 6.0 * f0) * c,
        f0 * c,
    )


STEP = 16
LANES = 128


def cosine_table(length):
    half = length // 2
    k = np.arange(half)
    weight = np.where(k == 0, 1.0, 2.0) / length
    phase = (k[:, None] * np.arange(length)[None, :]) % length
    return (np.cos(phase * (2.0 * np.pi / length)) * weight[:, None]).astype(np.float32)


def halves(v):
    high = v.astype(jnp.bfloat16)
    return high, (v - high.astype(jnp.float32)).astype(jnp.bfloat16)


def dot32(a, b):
    return jnp.dot(a, b, preferred_element_type=jnp.float32)


def transport_kernel(
    peers, groups,
    q_hbm, vx_ref, vy_ref, sx_ref, sy_ref, sc_ref, cos_hbm,
    out_ref,
    q_ref, cos_ref, line, th, tl, shift_of, place_of, wx, wy, part_hi, part_lo,
    ext, cols, col_hi, col_lo, turned, back, held, colv,
    sem_q, sem_c, sendx, recvx, sendv, recvv, send_up, send_down, recv_relay,
    send1, recv1, send2, recv2,
):
    ns, nz, rows, nx = q_ref.shape
    ny = rows * peers
    width = nx // peers
    ratio = peers // groups
    bx, by = nx // BLOCK, ny // BLOCK
    me = lax.axis_index("space")
    mine = lax.axis_index("scalar")
    home = me // ratio
    half = rows // 2
    parts = ((0, 0, half), (0, half, half), (1, 0, rows))

    def load(s, z):
        return pltpu.make_async_copy(q_hbm.at[s, z], q_ref.at[s, z], sem_q.at[s, z])

    tables = pltpu.make_async_copy(cos_hbm, cos_ref, sem_c)
    tables.start()
    for z in range(nz):
        for s in range(ns):
            load(s, z).start()

    barrier = pltpu.get_barrier_semaphore()
    for k in range(1, peers):
        pl.semaphore_signal(barrier, inc=1, device_id={"space": lax.rem(me + k, peers)}, device_id_type=MESH)
    for k in range(1, groups):
        pl.semaphore_signal(barrier, inc=1, device_id={"scalar": lax.rem(mine + k, groups)}, device_id_type=MESH)
    pl.semaphore_wait(barrier, peers + groups - 2)

    def spread(c, k):
        z, r, n = parts[c]
        return pltpu.make_async_remote_copy(
            src_ref=vx_ref.at[z, pl.ds(r, n), :], dst_ref=held.at[mine, z, pl.ds(r, n), :],
            send_sem=sendx.at[c, k - 1], recv_sem=recvx.at[c, k - 1],
            device_id={"scalar": lax.rem(mine + k, groups)}, device_id_type=MESH,
        )

    def collect(z, h):
        dest = ratio * mine + h
        k = lax.rem(dest - me + peers, peers)
        return pltpu.make_async_remote_copy(
            src_ref=vy_ref.at[z, :, pl.ds(h * width, width)], dst_ref=colv.at[z, me],
            send_sem=sendv.at[z, h], recv_sem=recvv.at[z, k],
            device_id={"space": dest}, device_id_type=MESH,
        )

    def collected(z, k):
        return pltpu.make_async_remote_copy(
            src_ref=vy_ref.at[z, :, pl.ds(0, width)], dst_ref=colv.at[z, me],
            send_sem=sendv.at[z, 0], recv_sem=recvv.at[z, k],
            device_id={"space": lax.rem(me + k, peers)}, device_id_type=MESH,
        )

    def relay(j, up):
        z, i = j // (peers // 2), j % (peers // 2)
        block = colv.at[z, pl.ds(2 * i, 2)]
        return pltpu.make_async_remote_copy(
            src_ref=block, dst_ref=block,
            send_sem=(send_up if up else send_down).at[j], recv_sem=recv_relay.at[j],
            device_id={"scalar": lax.rem(mine + (1 if up else groups - 1), groups)}, device_id_type=MESH,
        )

    goes_up = jnp.logical_and(mine >= home, mine < groups - 1)
    goes_down = jnp.logical_and(mine <= home, mine > 0)

    def pass_on(j):
        @pl.when(goes_up)
        def _():
            relay(j, True).start()

        @pl.when(goes_down)
        def _():
            relay(j, False).start()

    for k in range(1, groups):
        spread(0, k).start()
    for z in range(nz):
        for h in range(ratio):
            @pl.when(ratio * mine + h != me)
            def _():
                collect(z, h).start()

            @pl.when(ratio * mine + h == me)
            def _():
                colv[z, me] = vy_ref[z, :, h * width:(h + 1) * width]
    for c in range(1, len(parts)):
        for k in range(1, groups):
            spread(c, k).start()
    held[mine] = vx_ref[...]

    lane = lax.broadcasted_iota(jnp.int32, (rows, LANES), 1)
    for z in range(nz):
        shift = jnp.transpose(jnp.broadcast_to(sx_ref[z:z + 1, :] + REACH, (LANES, rows)))
        shift_of[z] = shift
        place_of[z] = (lane - shift) & (LANES - 1)

    top = nx // 2
    row = lax.broadcasted_iota(jnp.int32, (2 * ns, top), 0)
    index = jnp.full((2 * ns, top), sc_ref[0], jnp.int32)
    for s in range(1, ns):
        index = jnp.where(row % ns == s, sc_ref[s], index)
    rate = jnp.exp2((3 - index).astype(jnp.float32))
    rate = jnp.where(row < ns, 0.5 * rate, rate)
    relative = lax.broadcasted_iota(jnp.int32, (2 * ns, top), 1).astype(jnp.float32) / top
    damping = jnp.exp(-rate * relative * relative)
    tables.wait()
    g = jnp.dot(damping, cos_ref[...], precision=lax.Precision.HIGHEST, preferred_element_type=jnp.float32)
    last = jnp.exp(-rate[:, 0:1]) / nx
    odd = lax.broadcasted_iota(jnp.int32, (2 * ns, nx), 1) % 2
    g = g + jnp.where(odd == 1, -last, last)
    line[0:ns, :] = pltpu.roll(g, nx - (REACH + 2), 1)[0:ns]
    line[ns:, :] = pltpu.roll(g, REACH + 2, 1)[ns:]

    def circulant(t):
        for r in range(0, BLOCK, 64):
            wide = jnp.broadcast_to(line[pl.ds(t, 1), :], (64, nx))
            wide = pltpu.roll(wide, r, 1, stride=1, stride_axis=0)
            th[t, r:r + 64, :], tl[t, r:r + 64, :] = halves(wide)

    pl.loop(0, ns)(circulant)

    def weigh_rows(c):
        z, first_row, n = parts[c]
        for k in range(1, groups):
            spread(c, k).wait_recv()

        @pl.loop(0, n // 8)
        def _(i):
            at = pl.ds(pl.multiple_of(first_row + i * 8, 8), 8)
            f = jnp.concatenate([held[g, z, at, :] for g in range(groups)], axis=1)
            for m, w in enumerate(spline_weights(f)):
                wx[z, m, at, :] = pltpu.roll(w, m % 3, 1) if m % 3 else w

    def remesh_eight(z, at, q):
        one, two = pltpu.roll(q, 1, 1), pltpu.roll(q, 2, 1)
        near = q * wx[z, 0, at, :] + one * wx[z, 1, at, :] + two * wx[z, 2, at, :]
        far = q * wx[z, 3, at, :] + one * wx[z, 4, at, :] + two * wx[z, 5, at, :]
        total = near + pltpu.roll(far, 3, 1)
        place, shift = place_of[z, at, :], shift_of[z, at, :]
        stays = lax.broadcasted_iota(jnp.int32, shift.shape, 1) >= shift
        moved = [
            jnp.take_along_axis(total[:, v:v + LANES], place, axis=1) for v in range(0, nx, LANES)
        ]
        return jnp.concatenate(
            [jnp.where(stays, moved[v], moved[v - 1]) for v in range(nx // LANES)], axis=1
        )

    def remesh_rows(z, first_row, n, read):
        @pl.loop(0, n // STEP, unroll=2)
        def _(i):
            r = pl.multiple_of(first_row + i * STEP, STEP)
            both = [
                remesh_eight(z, pl.ds(pl.multiple_of(r + e, 8), 8), read(pl.ds(pl.multiple_of(r + e, 8), 8)))
                for e in (0, 8)
            ]
            at = pl.ds(r, STEP)
            part_hi[at, :], part_lo[at, :] = halves(jnp.concatenate(both, axis=0))

    def diffuse_rows(s, first_row, n, store):
        at = slice(first_row, first_row + n)
        for b in range(bx):
            total = jnp.zeros((n, BLOCK), jnp.float32)
            for a in range(bx):
                d = ((b - a) % bx) * BLOCK
                high, low = th[s, :, d:d + BLOCK], tl[s, :, d:d + BLOCK]
                left = part_hi[at, a * BLOCK:(a + 1) * BLOCK]
                rest = part_lo[at, a * BLOCK:(a + 1) * BLOCK]
                total = total + (dot32(left, high) + (dot32(left, low) + dot32(rest, high)))
            store(b, total)

    def forward(s, c, k):
        z, r, n = parts[c]
        dest = lax.rem(me + k, peers)
        return pltpu.make_async_remote_copy(
            src_ref=ext.at[s, z, dest, pl.ds(r, n), :], dst_ref=cols.at[s, z, me, pl.ds(r, n), :],
            send_sem=send1.at[s, c, k - 1], recv_sem=recv1.at[s, c, k - 1],
            device_id={"space": dest}, device_id_type=MESH,
        )

    def backward(s, z, k):
        dest = lax.rem(me + k, peers)
        return pltpu.make_async_remote_copy(
            src_ref=turned.at[s, dest, z], dst_ref=back.at[s, me, z],
            send_sem=send2.at[s, z, k - 1], recv_sem=recv2.at[s, z, k - 1],
            device_id={"space": dest}, device_id_type=MESH,
        )

    per = BLOCK // width

    def first_sweep(s, c):
        z, r, n = parts[c]
        remesh_rows(z, r, n, lambda at: q_ref[s, z, at, :])

        def store(b, total):
            for h in range(per):
                ext[s, z, b * per + h, r:r + n, :] = total[:, h * width:(h + 1) * width]

        diffuse_rows(s, r, n, store)
        for k in range(1, peers):
            forward(s, c, k).start()
        cols[s, z, me, r:r + n, :] = ext[s, z, me, r:r + n, :]

    def await_relay(j):
        @pl.when(mine != home)
        def _():
            relay(j, True).wait_recv()
            pass_on(j)

    count = nz * peers // 2
    for c in range(len(parts)):
        weigh_rows(c)

        @pl.loop(0, ns)
        def _(s):
            if parts[c][1] == 0:
                load(s, parts[c][0]).wait()
            first_sweep(s, c)
            if c == len(parts) - 1:
                await_relay(s)

        if c == 0:
            @pl.when(mine == home)
            def _():
                for z in range(nz):
                    for k in range(1, peers):
                        collected(z, k).wait_recv()

                    @pl.loop(z * (peers // 2), (z + 1) * (peers // 2))
                    def _(j):
                        pass_on(j)

    reach = 24
    part = 64

    def weigh_columns(z):
        @pl.loop(0, ny // part)
        def _(i):
            y = i * part
            before = lax.rem(y - 8 + ny, ny)
            f = jnp.concatenate(
                [
                    colv[z, before // rows, pl.ds(pl.multiple_of(before % rows, 8), 8), :],
                    colv[z, y // rows, pl.ds(pl.multiple_of(y % rows, part), part), :],
                ],
                axis=0,
            )
            for m, w in enumerate(spline_weights(f)):
                w = pltpu.roll(w, m % 3, 0) if m % 3 else w
                wy[z, m, pl.ds(pl.multiple_of(reach + y, 8), part), :] = w[8:]

        for m in range(6):
            wy[z, m, 0:reach, :] = wy[z, m, ny:ny + reach, :]

    @pl.loop(ns, count)
    def _(j):
        circulant(j)
        await_relay(j)

    for t in range(count, 2 * ns):
        circulant(t)
    for z in range(nz):
        weigh_columns(z)

    @pl.loop(0, ns)
    def _(s):
        for c in range(len(parts)):
            for k in range(1, peers):
                forward(s, c, k).wait_recv()

        @pl.loop(0, ny // part)
        def _(i):
            y = i * part
            before = lax.rem(y - reach + ny, ny)
            shift = sy_ref[...] + REACH
            for z in range(nz):
                q = jnp.concatenate(
                    [
                        cols[s, z, before // rows, pl.ds(pl.multiple_of(before % rows, 8), reach), :],
                        cols[s, z, y // rows, pl.ds(pl.multiple_of(y % rows, part), part), :],
                    ],
                    axis=0,
                )
                at = pl.ds(pl.multiple_of(y, part), reach + part)
                one, two = pltpu.roll(q, 1, 0), pltpu.roll(q, 2, 0)
                near = q * wy[z, 0, at, :] + one * wy[z, 1, at, :] + two * wy[z, 2, at, :]
                far = q * wy[z, 3, at, :] + one * wy[z, 4, at, :] + two * wy[z, 5, at, :]
                u = near + pltpu.roll(far, 3, 0)
                for bit in (1, 2, 4, 8, 16):
                    u = jnp.where((shift & bit) != 0, pltpu.roll(u, bit, 0), u)
                put = pl.ds(pl.multiple_of(y, part), part)
                lanes = slice(z * width, (z + 1) * width)
                col_hi[put, lanes], col_lo[put, lanes] = halves(u[reach:])

        for a in range(by):
            total = jnp.zeros((BLOCK, nz * width), jnp.float32)
            for b in range(by):
                d = ((b - a) % by) * BLOCK
                high, low = th[ns + s, :, d:d + BLOCK], tl[ns + s, :, d:d + BLOCK]
                left = col_hi[b * BLOCK:(b + 1) * BLOCK, :]
                rest = col_lo[b * BLOCK:(b + 1) * BLOCK, :]
                total = total + (dot32(high, left) + (dot32(low, left) + dot32(high, rest)))
            for h in range(BLOCK // rows):
                for z in range(nz):
                    turned[s, a * (BLOCK // rows) + h, z] = total[
                        h * rows:(h + 1) * rows, z * width:(z + 1) * width
                    ]
        for z in range(nz):
            for k in range(1, peers):
                backward(s, z, k).start()
        back[s, me] = turned[s, me]

    @pl.loop(0, ns)
    def _(s):
        for z in range(nz):
            for k in range(1, peers):
                backward(s, z, k).wait_recv()
            remesh_rows(
                z, 0, rows,
                lambda at: jnp.concatenate([back[s, p, z, at, :] for p in range(peers)], axis=1),
            )

            def store(b, total):
                out_ref[s, z, :, b * BLOCK:(b + 1) * BLOCK] = total

            diffuse_rows(s, 0, rows, store)

    @pl.loop(0, ns)
    def _(s):
        for k in range(1, peers):
            for c in range(len(parts)):
                forward(s, c, k).wait_send()
            for z in range(nz):
                backward(s, z, k).wait_send()

    for c in range(len(parts)):
        for k in range(1, groups):
            spread(c, k).wait_send()
    for z in range(nz):
        for h in range(ratio):
            @pl.when(ratio * mine + h != me)
            def _():
                collect(z, h).wait_send()

    @pl.loop(0, count)
    def _(j):
        @pl.when(goes_up)
        def _():
            relay(j, True).wait_send()

        @pl.when(goes_down)
        def _():
            relay(j, False).wait_send()


def transport_on_device(peers, groups, scalars, velocity_x, velocity_y, shift_x, shift_y, schmidt):
    ns, nz, rows, nx = scalars.shape
    ny, width = rows * peers, nx // peers
    f32, bf16, i32 = jnp.float32, jnp.bfloat16, jnp.int32
    vmem = pl.BlockSpec(memory_space=pltpu.VMEM)
    smem = pl.BlockSpec(memory_space=pltpu.SMEM)
    anywhere = pl.BlockSpec(memory_space=pl.ANY)
    count = nz * peers // 2
    dma = pltpu.SemaphoreType.DMA
    return pl.pallas_call(
        functools.partial(transport_kernel, peers, groups),
        out_shape=jax.ShapeDtypeStruct(scalars.shape, f32),
        in_specs=[anywhere, vmem, vmem, vmem, vmem, smem, anywhere],
        out_specs=vmem,
        scratch_shapes=[
            pltpu.VMEM(scalars.shape, f32),
            pltpu.VMEM((nx // 2, nx), f32),
            pltpu.VMEM((2 * ns, nx), f32),
            pltpu.VMEM((2 * ns, BLOCK, nx), bf16),
            pltpu.VMEM((2 * ns, BLOCK, nx), bf16),
            pltpu.VMEM((nz, rows, LANES), i32),
            pltpu.VMEM((nz, rows, LANES), i32),
            pltpu.VMEM((nz, 6, rows, nx), f32),
            pltpu.VMEM((nz, 6, ny + 24, width), f32),
            pltpu.VMEM((rows, nx), bf16),
            pltpu.VMEM((rows, nx), bf16),
            pltpu.VMEM((ns, nz, peers, rows, width), f32),
            pltpu.VMEM((ns, nz, peers, rows, width), f32),
            pltpu.VMEM((ny, nz * width), bf16),
            pltpu.VMEM((ny, nz * width), bf16),
            pltpu.VMEM((ns, peers, nz, rows, width), f32),
            pltpu.VMEM((ns, peers, nz, rows, width), f32),
            pltpu.VMEM((groups,) + velocity_x.shape, f32),
            pltpu.VMEM((nz, peers, rows, width), f32),
            dma((ns, nz)),
            dma,
            dma((3, groups - 1)),
            dma((3, groups - 1)),
            dma((nz, peers // groups)),
            dma((nz, peers)),
            dma((count,)),
            dma((count,)),
            dma((count,)),
            dma((ns, 3, peers - 1)),
            dma((ns, 3, peers - 1)),
            dma((ns, nz, peers - 1)),
            dma((ns, nz, peers - 1)),
        ],
        compiler_params=pltpu.CompilerParams(
            collective_id=0, has_side_effects=True, vmem_limit_bytes=60 * 2**20
        ),
    )(
        scalars, velocity_x, velocity_y, shift_x, shift_y[None, :], schmidt,
        jnp.asarray(cosine_table(nx)),
    )


def transport(peers, groups, scalars, *others):
    ns, nz, rows, nx = scalars.shape
    fits = (
        peers % groups == 0 and peers % 2 == 0 and nz == 2 and rows == LANES and nx == rows * peers == NY
        and ns <= nz * peers // 2 and others[0].shape[2] == nx // groups and nx % BLOCK == 0
    )
    if not fits:
        return on_device(scalars, *others)
    return transport_on_device(peers, groups, scalars, *others)


def solution(mesh):
    peers = mesh.shape["space"]
    body = functools.partial(transport, peers, mesh.shape["scalar"])
    return jax.shard_map(
        body,
        mesh=mesh,
        in_specs=(
            P("scalar", None, "space", None),
            P(None, "space", "scalar"),
            P(None, "space", "scalar"),
            P(None, "space"),
            P("space"),
            P("scalar"),
        ),
        out_specs=P("scalar", None, "space", None),
        check_vma=False,
    )
```

```python
import functools
import math

import jax
import jax.numpy as jnp
import numpy as np
from jax import lax
from jax.experimental import pallas as pl
from jax.experimental.pallas import tpu as pltpu
from jax.sharding import PartitionSpec as P

NY = 1024


def spline(distance):
    magnitude = jnp.abs(distance)
    far_part = jnp.maximum(3.0 - magnitude, 0.0)
    middle = jnp.maximum(2.0 - magnitude, 0.0)
    near_part = jnp.maximum(1.0 - magnitude, 0.0)
    return (far_part**5 - 6.0 * middle**5 + 15.0 * near_part**5) / 120.0


def remesh(fields, fraction, shift_line):
    summed = jnp.zeros_like(fields)
    for offset in range(-2, 4):
        weight = spline(offset - fraction)
        summed = summed + jnp.roll(fields * weight, offset, axis=-1)
    line_shift = shift_line[None, :, :, None]
    moved = summed
    for amount in range(-8, 9):
        moved = jnp.where(line_shift == amount, jnp.roll(summed, amount, axis=-1), moved)
    return moved


def remesh_columns(fields, fraction, shift_cols):
    summed = jnp.zeros_like(fields)
    for offset in range(-2, 4):
        weight = spline(offset - fraction)
        summed = summed + jnp.roll(fields * weight[None], offset, axis=2)
    column_shift = shift_cols[None, None, None, :]
    moved = summed
    for amount in range(-8, 9):
        moved = jnp.where(column_shift == amount, jnp.roll(summed, amount, axis=2), moved)
    return moved


def spectral_tables(length):
    midpoint = length // 2
    column = jnp.arange(length, dtype=jnp.int32)
    wavenum = jnp.where(column <= midpoint, column, column - midpoint)
    phases = column[:, None] * wavenum[None, :] % length
    angles = phases.astype(jnp.float32) * (2.0 * math.pi / length)
    forward = jnp.where((column <= midpoint)[None, :], jnp.cos(angles), jnp.sin(angles))
    inverse_weight = jnp.where((wavenum == 0) | (column == midpoint), 1.0, 2.0) / length
    inverse = forward.T * inverse_weight[:, None]
    relative = wavenum.astype(jnp.float32) / midpoint
    return (forward, inverse, relative * relative)


def diffuse(fields, diffusivity, tables):
    forward, inverse, wave_square = tables
    initial = fields.shape
    rows_flat = fields.reshape(-1, initial[-1])
    spectra = jnp.dot(
        rows_flat, forward, precision=lax.Precision.HIGHEST, preferred_element_type=jnp.float32
    )
    damping = jnp.exp(-diffusivity[:, None] * wave_square[None, :])
    spectra = spectra.reshape(initial) * damping[:, None, None, :]
    result = jnp.dot(
        spectra.reshape(-1, initial[-1]),
        inverse,
        precision=lax.Precision.HIGHEST,
        preferred_element_type=jnp.float32,
    )
    return result.reshape(initial)


def diffuse_columns(fields, diffusivity, tables):
    forward, inverse, wave_square = tables
    spectra = jnp.einsum(
        "jk,szjx->szkx",
        forward,
        fields,
        precision=lax.Precision.HIGHEST,
        preferred_element_type=jnp.float32,
    )
    damping = jnp.exp(-diffusivity[:, None] * wave_square[None, :])
    spectra = spectra * damping[:, None, :, None]
    return jnp.einsum(
        "kj,szkx->szjx",
        inverse,
        spectra,
        precision=lax.Precision.HIGHEST,
        preferred_element_type=jnp.float32,
    )


def one_sweep(fields, fraction, shift_line, diffusivity, tables):
    return diffuse(remesh(fields, fraction, shift_line), diffusivity, tables)


def fetch_velocity(velocity_x):
    return lax.all_gather(velocity_x, "scalar", axis=2, tiled=True)


def on_device(scalars, velocity_x, velocity_y, shift_x, shift_y, schmidt):
    diffusivity = jnp.exp2((3 - schmidt).astype(jnp.float32))
    tables_x = spectral_tables(scalars.shape[3])
    tables_y = spectral_tables(NY)
    along_x = fetch_velocity(velocity_x)
    fields = one_sweep(scalars, along_x, shift_x, 0.5 * diffusivity, tables_x)
    along_y = lax.all_gather(velocity_y, "scalar", axis=2, tiled=True)
    fields_cols, velocity_cols = (
        lax.all_to_all(fields, "space", split_axis=3, concat_axis=2, tiled=True),
        lax.all_to_all(along_y[None], "space", split_axis=3, concat_axis=2, tiled=True),
    )
    remeshed = remesh_columns(fields_cols, velocity_cols[0], shift_y)
    returned = diffuse_columns(remeshed, diffusivity, tables_y)
    fields = lax.all_to_all(returned, "space", split_axis=2, concat_axis=3, tiled=True)
    along_x = fetch_velocity(velocity_x)
    return one_sweep(fields, along_x, shift_x, 0.5 * diffusivity, tables_x)


BLOCK = 256
REACH = 8
MESH = pl.DeviceIdType.MESH


def spline_weights(f):
    g = 1.0 - f

    def fifth(v):
        w = v * v
        return w * w * v

    f0, f1, f2 = fifth(f), fifth(1.0 + f), fifth(2.0 + f)
    g0, g1, g2 = fifth(g), fifth(1.0 + g), fifth(2.0 + g)
    c = 1.0 / 120.0
    return (
        g0 * c,
        (g1 - 6.0 * g0) * c,
        (g2 - 6.0 * g1 + 15.0 * g0) * c,
        (f2 - 6.0 * f1 + 15.0 * f0) * c,
        (f1 - 6.0 * f0) * c,
        f0 * c,
    )


STEP = 16
LANES = 128


def cosine_table(length):
    half = length // 2
    k = np.arange(half)
    weight = np.where(k == 0, 1.0, 2.0) / length
    phase = (k[:, None] * np.arange(length)[None, :]) % length
    return (np.cos(phase * (2.0 * np.pi / length)) * weight[:, None]).astype(np.float32)


def halves(v):
    high = v.astype(jnp.bfloat16)
    return high, (v - high.astype(jnp.float32)).astype(jnp.bfloat16)


def dot32(a, b):
    return jnp.dot(a, b, preferred_element_type=jnp.float32)


def transport_kernel(
    peers, groups,
    q_hbm, vx_ref, vy_ref, sx_ref, sy_ref, sc_ref, cos_hbm,
    out_ref,
    q_ref, cos_ref, line, th, tl, shift_of, place_of, wx, wy, part_hi, part_lo,
    ext, cols, col_hi, col_lo, turned, back, held, colv,
    sem_q, sem_c, sendx, recvx, sendv, recvv, send_up, send_down, recv_relay,
    send1, recv1, send2, recv2,
):
    ns, nz, rows, nx = q_ref.shape
    ny = rows * peers
    width = nx // peers
    ratio = peers // groups
    bx, by = nx // BLOCK, ny // BLOCK
    me = lax.axis_index("space")
    mine = lax.axis_index("scalar")
    home = me // ratio
    half = rows // 2
    parts = ((0, 0, half), (0, half, half), (1, 0, rows))

    def load(s, z):
        return pltpu.make_async_copy(q_hbm.at[s, z], q_ref.at[s, z], sem_q.at[s, z])

    tables = pltpu.make_async_copy(cos_hbm, cos_ref, sem_c)
    tables.start()
    for z in range(nz):
        for s in range(ns):
            load(s, z).start()

    barrier = pltpu.get_barrier_semaphore()
    for k in range(1, peers):
        pl.semaphore_signal(barrier, inc=1, device_id={"space": lax.rem(me + k, peers)}, device_id_type=MESH)
    for k in range(1, groups):
        pl.semaphore_signal(barrier, inc=1, device_id={"scalar": lax.rem(mine + k, groups)}, device_id_type=MESH)
    pl.semaphore_wait(barrier, peers + groups - 2)

    def spread(c, k):
        z, r, n = parts[c]
        return pltpu.make_async_remote_copy(
            src_ref=vx_ref.at[z, pl.ds(r, n), :], dst_ref=held.at[mine, z, pl.ds(r, n), :],
            send_sem=sendx.at[c, k - 1], recv_sem=recvx.at[c, k - 1],
            device_id={"scalar": lax.rem(mine + k, groups)}, device_id_type=MESH,
        )

    def collect(z, h):
        dest = ratio * mine + h
        k = lax.rem(dest - me + peers, peers)
        return pltpu.make_async_remote_copy(
            src_ref=vy_ref.at[z, :, pl.ds(h * width, width)], dst_ref=colv.at[z, me],
            send_sem=sendv.at[z, h], recv_sem=recvv.at[z, k],
            device_id={"space": dest}, device_id_type=MESH,
        )

    def collected(z, k):
        return pltpu.make_async_remote_copy(
            src_ref=vy_ref.at[z, :, pl.ds(0, width)], dst_ref=colv.at[z, me],
            send_sem=sendv.at[z, 0], recv_sem=recvv.at[z, k],
            device_id={"space": lax.rem(me + k, peers)}, device_id_type=MESH,
        )

    def relay(j, up):
        z, i = j // (peers // 2), j % (peers // 2)
        block = colv.at[z, pl.ds(2 * i, 2)]
        return pltpu.make_async_remote_copy(
            src_ref=block, dst_ref=block,
            send_sem=(send_up if up else send_down).at[j], recv_sem=recv_relay.at[j],
            device_id={"scalar": lax.rem(mine + (1 if up else groups - 1), groups)}, device_id_type=MESH,
        )

    goes_up = jnp.logical_and(mine >= home, mine < groups - 1)
    goes_down = jnp.logical_and(mine <= home, mine > 0)

    def pass_on(j):
        @pl.when(goes_up)
        def _():
            relay(j, True).start()

        @pl.when(goes_down)
        def _():
            relay(j, False).start()

    for k in range(1, groups):
        spread(0, k).start()
    for z in range(nz):
        for h in range(ratio):
            @pl.when(ratio * mine + h != me)
            def _():
                collect(z, h).start()

            @pl.when(ratio * mine + h == me)
            def _():
                colv[z, me] = vy_ref[z, :, h * width:(h + 1) * width]
    for c in range(1, len(parts)):
        for k in range(1, groups):
            spread(c, k).start()
    held[mine] = vx_ref[...]

    lane = lax.broadcasted_iota(jnp.int32, (rows, LANES), 1)
    for z in range(nz):
        shift = jnp.transpose(jnp.broadcast_to(sx_ref[z:z + 1, :] + REACH, (LANES, rows)))
        shift_of[z] = shift
        place_of[z] = (lane - shift) & (LANES - 1)

    top = nx // 2
    row = lax.broadcasted_iota(jnp.int32, (2 * ns, top), 0)
    index = jnp.full((2 * ns, top), sc_ref[0], jnp.int32)
    for s in range(1, ns):
        index = jnp.where(row % ns == s, sc_ref[s], index)
    rate = jnp.exp2((3 - index).astype(jnp.float32))
    rate = jnp.where(row < ns, 0.5 * rate, rate)
    relative = lax.broadcasted_iota(jnp.int32, (2 * ns, top), 1).astype(jnp.float32) / top
    damping = jnp.exp(-rate * relative * relative)
    tables.wait()
    g = jnp.dot(damping, cos_ref[...], precision=lax.Precision.HIGHEST, preferred_element_type=jnp.float32)
    last = jnp.exp(-rate[:, 0:1]) / nx
    odd = lax.broadcasted_iota(jnp.int32, (2 * ns, nx), 1) % 2
    g = g + jnp.where(odd == 1, -last, last)
    line[0:ns, :] = pltpu.roll(g, nx - (REACH + 2), 1)[0:ns]
    line[ns:, :] = pltpu.roll(g, REACH + 2, 1)[ns:]

    def circulant(t):
        for r in range(0, LANES, 64):
            wide = jnp.broadcast_to(line[pl.ds(t, 1), :], (64, nx))
            high, low = halves(pltpu.roll(wide, r, 1, stride=1, stride_axis=0))
            for e in range(0, BLOCK, LANES):
                at = slice(r + e, r + e + 64)
                th[t, at, e:], tl[t, at, e:] = high[:, :nx - e], low[:, :nx - e]
                if e:
                    th[t, at, :e], tl[t, at, :e] = high[:, nx - e:], low[:, nx - e:]

    circulant(0)

    def weigh_rows(c):
        z, first_row, n = parts[c]
        for k in range(1, groups):
            spread(c, k).wait_recv()

        @pl.loop(0, n // 8, unroll=2)
        def _(i):
            at = pl.ds(pl.multiple_of(first_row + i * 8, 8), 8)
            f = jnp.concatenate([held[g, z, at, :] for g in range(groups)], axis=1)
            for m, w in enumerate(spline_weights(f)):
                wx[z, m, at, :] = pltpu.roll(w, m % 3, 1) if m % 3 else w

    def remesh_eight(z, at, q):
        one, two = pltpu.roll(q, 1, 1), pltpu.roll(q, 2, 1)
        near = q * wx[z, 0, at, :] + one * wx[z, 1, at, :] + two * wx[z, 2, at, :]
        far = q * wx[z, 3, at, :] + one * wx[z, 4, at, :] + two * wx[z, 5, at, :]
        total = near + pltpu.roll(far, 3, 1)
        place, shift = place_of[z, at, :], shift_of[z, at, :]
        stays = lax.broadcasted_iota(jnp.int32, shift.shape, 1) >= shift
        moved = [
            jnp.take_along_axis(total[:, v:v + LANES], place, axis=1) for v in range(0, nx, LANES)
        ]
        return jnp.concatenate(
            [jnp.where(stays, moved[v], moved[v - 1]) for v in range(nx // LANES)], axis=1
        )

    def remesh_rows(z, first_row, n, read):
        @pl.loop(0, n // STEP, unroll=2)
        def _(i):
            r = pl.multiple_of(first_row + i * STEP, STEP)
            both = [
                remesh_eight(z, pl.ds(pl.multiple_of(r + e, 8), 8), read(pl.ds(pl.multiple_of(r + e, 8), 8)))
                for e in (0, 8)
            ]
            at = pl.ds(r, STEP)
            part_hi[at, :], part_lo[at, :] = halves(jnp.concatenate(both, axis=0))

    def diffuse_rows(s, first_row, n, store):
        at = slice(first_row, first_row + n)
        for b in range(bx):
            turns = [((b - a) % bx) * BLOCK for a in range(bx)]
            high = jnp.concatenate([th[s, :, d:d + BLOCK] for d in turns], axis=0)
            low = jnp.concatenate([tl[s, :, d:d + BLOCK] for d in turns], axis=0)
            left = part_hi[at, :]
            both = dot32(jnp.concatenate([left, part_lo[at, :]], axis=0), high)
            store(b, both[:n] + (dot32(left, low) + both[n:]))

    def forward(s, c, k):
        z, r, n = parts[c]
        dest = lax.rem(me + k, peers)
        return pltpu.make_async_remote_copy(
            src_ref=ext.at[s, z, dest, pl.ds(r, n), :], dst_ref=cols.at[s, z, me, pl.ds(r, n), :],
            send_sem=send1.at[s, c, k - 1], recv_sem=recv1.at[s, c, k - 1],
            device_id={"space": dest}, device_id_type=MESH,
        )

    def backward(s, z, k):
        dest = lax.rem(me + k, peers)
        return pltpu.make_async_remote_copy(
            src_ref=turned.at[s, dest, z], dst_ref=back.at[s, me, z],
            send_sem=send2.at[s, z, k - 1], recv_sem=recv2.at[s, z, k - 1],
            device_id={"space": dest}, device_id_type=MESH,
        )

    per = BLOCK // width

    def first_sweep(s, c):
        z, r, n = parts[c]
        remesh_rows(z, r, n, lambda at: q_ref[s, z, at, :])

        def store(b, total):
            for h in range(per):
                ext[s, z, b * per + h, r:r + n, :] = total[:, h * width:(h + 1) * width]

        diffuse_rows(s, r, n, store)
        for k in range(1, peers):
            forward(s, c, k).start()
        cols[s, z, me, r:r + n, :] = ext[s, z, me, r:r + n, :]

    def await_relay(j):
        @pl.when(mine != home)
        def _():
            relay(j, True).wait_recv()
            pass_on(j)

    count = nz * peers // 2
    for c in range(len(parts)):
        weigh_rows(c)

        @pl.loop(0, ns)
        def _(s):
            if parts[c][1] == 0:
                load(s, parts[c][0]).wait()
            first_sweep(s, c)
            if c == 0:
                circulant(s + 1)
            if c == len(parts) - 1:
                await_relay(s)

        if c == 0:
            @pl.when(mine == home)
            def _():
                for z in range(nz):
                    for k in range(1, peers):
                        collected(z, k).wait_recv()

                    @pl.loop(z * (peers // 2), (z + 1) * (peers // 2))
                    def _(j):
                        pass_on(j)

    reach = 24
    part = 64

    def weigh_columns(z):
        @pl.loop(0, ny // part)
        def _(i):
            y = i * part
            before = lax.rem(y - 8 + ny, ny)
            f = jnp.concatenate(
                [
                    colv[z, before // rows, pl.ds(pl.multiple_of(before % rows, 8), 8), :],
                    colv[z, y // rows, pl.ds(pl.multiple_of(y % rows, part), part), :],
                ],
                axis=0,
            )
            for m, w in enumerate(spline_weights(f)):
                w = pltpu.roll(w, m % 3, 0) if m % 3 else w
                wy[z, m, pl.ds(pl.multiple_of(reach + y, 8), part), :] = w[8:]

        for m in range(6):
            wy[z, m, 0:reach, :] = wy[z, m, ny:ny + reach, :]

    weigh_columns(0)

    @pl.loop(ns, count)
    def _(j):
        await_relay(j)

        @pl.when(j < 2 * ns - 1)
        def _():
            circulant(j + 1)

    for t in range(count + 1, 2 * ns):
        circulant(t)
    for z in range(1, nz):
        weigh_columns(z)

    @pl.loop(0, ns)
    def _(s):
        for c in range(len(parts)):
            for k in range(1, peers):
                forward(s, c, k).wait_recv()

        @pl.loop(0, ny // part)
        def _(i):
            y = i * part
            before = lax.rem(y - reach + ny, ny)
            shift = sy_ref[...] + REACH
            for z in range(nz):
                q = jnp.concatenate(
                    [
                        cols[s, z, before // rows, pl.ds(pl.multiple_of(before % rows, 8), reach), :],
                        cols[s, z, y // rows, pl.ds(pl.multiple_of(y % rows, part), part), :],
                    ],
                    axis=0,
                )
                at = pl.ds(pl.multiple_of(y, part), reach + part)
                one, two = pltpu.roll(q, 1, 0), pltpu.roll(q, 2, 0)
                near = q * wy[z, 0, at, :] + one * wy[z, 1, at, :] + two * wy[z, 2, at, :]
                far = q * wy[z, 3, at, :] + one * wy[z, 4, at, :] + two * wy[z, 5, at, :]
                u = near + pltpu.roll(far, 3, 0)
                for bit in (1, 2, 4, 8, 16):
                    u = jnp.where((shift & bit) != 0, pltpu.roll(u, bit, 0), u)
                put = pl.ds(pl.multiple_of(y, part), part)
                lanes = slice(z * width, (z + 1) * width)
                col_hi[put, lanes], col_lo[put, lanes] = halves(u[reach:])

        for a in range(by):
            total = jnp.zeros((BLOCK, nz * width), jnp.float32)
            for b in range(by):
                d = ((b - a) % by) * BLOCK
                high, low = th[ns + s, :, d:d + BLOCK], tl[ns + s, :, d:d + BLOCK]
                left = col_hi[b * BLOCK:(b + 1) * BLOCK, :]
                rest = col_lo[b * BLOCK:(b + 1) * BLOCK, :]
                total = total + (dot32(high, left) + (dot32(low, left) + dot32(high, rest)))
            for h in range(BLOCK // rows):
                for z in range(nz):
                    turned[s, a * (BLOCK // rows) + h, z] = total[
                        h * rows:(h + 1) * rows, z * width:(z + 1) * width
                    ]
        for z in range(nz):
            for k in range(1, peers):
                backward(s, z, k).start()
        back[s, me] = turned[s, me]

    @pl.loop(0, ns)
    def _(s):
        for z in range(nz):
            for k in range(1, peers):
                backward(s, z, k).wait_recv()
            remesh_rows(
                z, 0, rows,
                lambda at: jnp.concatenate([back[s, p, z, at, :] for p in range(peers)], axis=1),
            )

            def store(b, total):
                out_ref[s, z, :, b * BLOCK:(b + 1) * BLOCK] = total

            diffuse_rows(s, 0, rows, store)

    @pl.loop(0, ns)
    def _(s):
        for k in range(1, peers):
            for c in range(len(parts)):
                forward(s, c, k).wait_send()
            for z in range(nz):
                backward(s, z, k).wait_send()

    for c in range(len(parts)):
        for k in range(1, groups):
            spread(c, k).wait_send()
    for z in range(nz):
        for h in range(ratio):
            @pl.when(ratio * mine + h != me)
            def _():
                collect(z, h).wait_send()

    @pl.loop(0, count)
    def _(j):
        @pl.when(goes_up)
        def _():
            relay(j, True).wait_send()

        @pl.when(goes_down)
        def _():
            relay(j, False).wait_send()


def hand_over_kernel(held_ref, out_ref, sem):
    copies = [
        pltpu.make_async_copy(held_ref.at[s], out_ref.at[s], sem.at[s]) for s in range(held_ref.shape[0])
    ]
    for copy in copies:
        copy.start()
    for copy in copies:
        copy.wait()


def transport_on_device(peers, groups, scalars, velocity_x, velocity_y, shift_x, shift_y, schmidt):
    ns, nz, rows, nx = scalars.shape
    ny, width = rows * peers, nx // peers
    f32, bf16, i32 = jnp.float32, jnp.bfloat16, jnp.int32
    vmem = pl.BlockSpec(memory_space=pltpu.VMEM)
    smem = pl.BlockSpec(memory_space=pltpu.SMEM)
    anywhere = pl.BlockSpec(memory_space=pl.ANY)
    count = nz * peers // 2
    dma = pltpu.SemaphoreType.DMA
    result = pl.pallas_call(
        functools.partial(transport_kernel, peers, groups),
        out_shape=pltpu.VMEM(scalars.shape, f32),
        in_specs=[anywhere, vmem, vmem, vmem, vmem, smem, anywhere],
        out_specs=vmem,
        scratch_shapes=[
            pltpu.VMEM(scalars.shape, f32),
            pltpu.VMEM((nx // 2, nx), f32),
            pltpu.VMEM((2 * ns, nx), f32),
            pltpu.VMEM((2 * ns, BLOCK, nx), bf16),
            pltpu.VMEM((2 * ns, BLOCK, nx), bf16),
            pltpu.VMEM((nz, rows, LANES), i32),
            pltpu.VMEM((nz, rows, LANES), i32),
            pltpu.VMEM((nz, 6, rows, nx), f32),
            pltpu.VMEM((nz, 6, ny + 24, width), f32),
            pltpu.VMEM((rows, nx), bf16),
            pltpu.VMEM((rows, nx), bf16),
            pltpu.VMEM((ns, nz, peers, rows, width), f32),
            pltpu.VMEM((ns, nz, peers, rows, width), f32),
            pltpu.VMEM((ny, nz * width), bf16),
            pltpu.VMEM((ny, nz * width), bf16),
            pltpu.VMEM((ns, peers, nz, rows, width), f32),
            pltpu.VMEM((ns, peers, nz, rows, width), f32),
            pltpu.VMEM((groups,) + velocity_x.shape, f32),
            pltpu.VMEM((nz, peers, rows, width), f32),
            dma((ns, nz)),
            dma,
            dma((3, groups - 1)),
            dma((3, groups - 1)),
            dma((nz, peers // groups)),
            dma((nz, peers)),
            dma((count,)),
            dma((count,)),
            dma((count,)),
            dma((ns, 3, peers - 1)),
            dma((ns, 3, peers - 1)),
            dma((ns, nz, peers - 1)),
            dma((ns, nz, peers - 1)),
        ],
        compiler_params=pltpu.CompilerParams(
            collective_id=0, has_side_effects=True, vmem_limit_bytes=52 * 2**20
        ),
    )(
        scalars, velocity_x, velocity_y, shift_x, shift_y[None, :], schmidt,
        jnp.asarray(cosine_table(nx)),
    )
    return pl.pallas_call(
        hand_over_kernel,
        out_shape=jax.ShapeDtypeStruct(scalars.shape, f32),
        in_specs=[anywhere],
        out_specs=anywhere,
        scratch_shapes=[dma((ns,))],
        compiler_params=pltpu.CompilerParams(vmem_limit_bytes=2**20),
    )(result)


def transport(peers, groups, scalars, *others):
    ns, nz, rows, nx = scalars.shape
    fits = (
        peers % groups == 0 and peers % 2 == 0 and nz == 2 and rows == LANES and nx == rows * peers == NY
        and ns <= nz * peers // 2 and others[0].shape[2] == nx // groups and nx % BLOCK == 0
    )
    if not fits:
        return on_device(scalars, *others)
    return transport_on_device(peers, groups, scalars, *others)


def solution(mesh):
    peers = mesh.shape["space"]
    body = functools.partial(transport, peers, mesh.shape["scalar"])
    return jax.shard_map(
        body,
        mesh=mesh,
        in_specs=(
            P("scalar", None, "space", None),
            P(None, "space", "scalar"),
            P(None, "space", "scalar"),
            P(None, "space"),
            P("space"),
            P("scalar"),
        ),
        out_specs=P("scalar", None, "space", None),
        check_vma=False,
    )
```

```python
import functools
import math

import jax
import jax.numpy as jnp
import numpy as np
from jax import lax
from jax.experimental import pallas as pl
from jax.experimental.pallas import tpu as pltpu
from jax.sharding import PartitionSpec as P

NY = 1024


def spline(distance):
    magnitude = jnp.abs(distance)
    far_part = jnp.maximum(3.0 - magnitude, 0.0)
    middle = jnp.maximum(2.0 - magnitude, 0.0)
    near_part = jnp.maximum(1.0 - magnitude, 0.0)
    return (far_part**5 - 6.0 * middle**5 + 15.0 * near_part**5) / 120.0


def remesh(fields, fraction, shift_line):
    summed = jnp.zeros_like(fields)
    for offset in range(-2, 4):
        weight = spline(offset - fraction)
        summed = summed + jnp.roll(fields * weight, offset, axis=-1)
    line_shift = shift_line[None, :, :, None]
    moved = summed
    for amount in range(-8, 9):
        moved = jnp.where(line_shift == amount, jnp.roll(summed, amount, axis=-1), moved)
    return moved


def remesh_columns(fields, fraction, shift_cols):
    summed = jnp.zeros_like(fields)
    for offset in range(-2, 4):
        weight = spline(offset - fraction)
        summed = summed + jnp.roll(fields * weight[None], offset, axis=2)
    column_shift = shift_cols[None, None, None, :]
    moved = summed
    for amount in range(-8, 9):
        moved = jnp.where(column_shift == amount, jnp.roll(summed, amount, axis=2), moved)
    return moved


def spectral_tables(length):
    midpoint = length // 2
    column = jnp.arange(length, dtype=jnp.int32)
    wavenum = jnp.where(column <= midpoint, column, column - midpoint)
    phases = column[:, None] * wavenum[None, :] % length
    angles = phases.astype(jnp.float32) * (2.0 * math.pi / length)
    forward = jnp.where((column <= midpoint)[None, :], jnp.cos(angles), jnp.sin(angles))
    inverse_weight = jnp.where((wavenum == 0) | (column == midpoint), 1.0, 2.0) / length
    inverse = forward.T * inverse_weight[:, None]
    relative = wavenum.astype(jnp.float32) / midpoint
    return (forward, inverse, relative * relative)


def diffuse(fields, diffusivity, tables):
    forward, inverse, wave_square = tables
    initial = fields.shape
    rows_flat = fields.reshape(-1, initial[-1])
    spectra = jnp.dot(
        rows_flat, forward, precision=lax.Precision.HIGHEST, preferred_element_type=jnp.float32
    )
    damping = jnp.exp(-diffusivity[:, None] * wave_square[None, :])
    spectra = spectra.reshape(initial) * damping[:, None, None, :]
    result = jnp.dot(
        spectra.reshape(-1, initial[-1]),
        inverse,
        precision=lax.Precision.HIGHEST,
        preferred_element_type=jnp.float32,
    )
    return result.reshape(initial)


def diffuse_columns(fields, diffusivity, tables):
    forward, inverse, wave_square = tables
    spectra = jnp.einsum(
        "jk,szjx->szkx",
        forward,
        fields,
        precision=lax.Precision.HIGHEST,
        preferred_element_type=jnp.float32,
    )
    damping = jnp.exp(-diffusivity[:, None] * wave_square[None, :])
    spectra = spectra * damping[:, None, :, None]
    return jnp.einsum(
        "kj,szkx->szjx",
        inverse,
        spectra,
        precision=lax.Precision.HIGHEST,
        preferred_element_type=jnp.float32,
    )


def one_sweep(fields, fraction, shift_line, diffusivity, tables):
    return diffuse(remesh(fields, fraction, shift_line), diffusivity, tables)


def fetch_velocity(velocity_x):
    return lax.all_gather(velocity_x, "scalar", axis=2, tiled=True)


def on_device(scalars, velocity_x, velocity_y, shift_x, shift_y, schmidt):
    diffusivity = jnp.exp2((3 - schmidt).astype(jnp.float32))
    tables_x = spectral_tables(scalars.shape[3])
    tables_y = spectral_tables(NY)
    along_x = fetch_velocity(velocity_x)
    fields = one_sweep(scalars, along_x, shift_x, 0.5 * diffusivity, tables_x)
    along_y = lax.all_gather(velocity_y, "scalar", axis=2, tiled=True)
    fields_cols, velocity_cols = (
        lax.all_to_all(fields, "space", split_axis=3, concat_axis=2, tiled=True),
        lax.all_to_all(along_y[None], "space", split_axis=3, concat_axis=2, tiled=True),
    )
    remeshed = remesh_columns(fields_cols, velocity_cols[0], shift_y)
    returned = diffuse_columns(remeshed, diffusivity, tables_y)
    fields = lax.all_to_all(returned, "space", split_axis=2, concat_axis=3, tiled=True)
    along_x = fetch_velocity(velocity_x)
    return one_sweep(fields, along_x, shift_x, 0.5 * diffusivity, tables_x)


BLOCK = 256
REACH = 8
MESH = pl.DeviceIdType.MESH


def spline_weights(f):
    g = 1.0 - f

    def fifth(v):
        w = v * v
        return w * w * v

    f0, f1, f2 = fifth(f), fifth(1.0 + f), fifth(2.0 + f)
    g0, g1, g2 = fifth(g), fifth(1.0 + g), fifth(2.0 + g)
    c = 1.0 / 120.0
    return (
        g0 * c,
        (g1 - 6.0 * g0) * c,
        (g2 - 6.0 * g1 + 15.0 * g0) * c,
        (f2 - 6.0 * f1 + 15.0 * f0) * c,
        (f1 - 6.0 * f0) * c,
        f0 * c,
    )


STEP = 16
LANES = 128


def cosine_table(length):
    half = length // 2
    k = np.arange(half)
    weight = np.where(k == 0, 1.0, 2.0) / length
    phase = (k[:, None] * np.arange(length)[None, :]) % length
    return (np.cos(phase * (2.0 * np.pi / length)) * weight[:, None]).astype(np.float32)


def halves(v):
    high = v.astype(jnp.bfloat16)
    return high, (v - high.astype(jnp.float32)).astype(jnp.bfloat16)


def dot32(a, b):
    return jnp.dot(a, b, preferred_element_type=jnp.float32)


def diffuse_rows(part_hi, part_lo, th, tl, s, first_row, n, store):
    at = slice(first_row, first_row + n)
    blocks = part_hi.shape[1] // BLOCK
    for b in range(blocks):
        turns = [((b - a) % blocks) * BLOCK for a in range(blocks)]
        high = jnp.concatenate([th[s, :, d:d + BLOCK] for d in turns], axis=0)
        low = jnp.concatenate([tl[s, :, d:d + BLOCK] for d in turns], axis=0)
        left = part_hi[at, :]
        both = dot32(jnp.concatenate([left, part_lo[at, :]], axis=0), high)
        store(b, both[:n] + (dot32(left, low) + both[n:]))


def transport_kernel(
    peers, groups,
    q_hbm, vx_ref, vy_ref, sx_ref, sy_ref, sc_ref, cos_hbm,
    out_ref, th, tl, part_hi, part_lo,
    q_ref, cos_ref, line, shift_of, place_of, wx, wy,
    ext, cols, col_hi, col_lo, turned, back, held, colv,
    sem_q, sem_c, sendx, recvx, sendv, recvv, send_up, send_down, recv_relay,
    send1, recv1, send2, recv2,
):
    ns, nz, rows, nx = q_ref.shape
    ny = rows * peers
    width = nx // peers
    ratio = peers // groups
    bx, by = nx // BLOCK, ny // BLOCK
    me = lax.axis_index("space")
    mine = lax.axis_index("scalar")
    home = me // ratio
    half = rows // 2
    parts = ((0, 0, half), (0, half, half), (1, 0, rows))

    def load(s, z):
        return pltpu.make_async_copy(q_hbm.at[s, z], q_ref.at[s, z], sem_q.at[s, z])

    tables = pltpu.make_async_copy(cos_hbm, cos_ref, sem_c)
    tables.start()
    for z in range(nz):
        for s in range(ns):
            load(s, z).start()

    barrier = pltpu.get_barrier_semaphore()
    for k in range(1, peers):
        pl.semaphore_signal(barrier, inc=1, device_id={"space": lax.rem(me + k, peers)}, device_id_type=MESH)
    for k in range(1, groups):
        pl.semaphore_signal(barrier, inc=1, device_id={"scalar": lax.rem(mine + k, groups)}, device_id_type=MESH)
    pl.semaphore_wait(barrier, peers + groups - 2)

    def spread(c, k):
        z, r, n = parts[c]
        return pltpu.make_async_remote_copy(
            src_ref=vx_ref.at[z, pl.ds(r, n), :], dst_ref=held.at[mine, z, pl.ds(r, n), :],
            send_sem=sendx.at[c, k - 1], recv_sem=recvx.at[c, k - 1],
            device_id={"scalar": lax.rem(mine + k, groups)}, device_id_type=MESH,
        )

    def collect(z, h):
        dest = ratio * mine + h
        k = lax.rem(dest - me + peers, peers)
        return pltpu.make_async_remote_copy(
            src_ref=vy_ref.at[z, :, pl.ds(h * width, width)], dst_ref=colv.at[z, me],
            send_sem=sendv.at[z, h], recv_sem=recvv.at[z, k],
            device_id={"space": dest}, device_id_type=MESH,
        )

    def collected(z, k):
        return pltpu.make_async_remote_copy(
            src_ref=vy_ref.at[z, :, pl.ds(0, width)], dst_ref=colv.at[z, me],
            send_sem=sendv.at[z, 0], recv_sem=recvv.at[z, k],
            device_id={"space": lax.rem(me + k, peers)}, device_id_type=MESH,
        )

    def relay(j, up):
        z, i = j // (peers // 2), j % (peers // 2)
        block = colv.at[z, pl.ds(2 * i, 2)]
        return pltpu.make_async_remote_copy(
            src_ref=block, dst_ref=block,
            send_sem=(send_up if up else send_down).at[j], recv_sem=recv_relay.at[j],
            device_id={"scalar": lax.rem(mine + (1 if up else groups - 1), groups)}, device_id_type=MESH,
        )

    goes_up = jnp.logical_and(mine >= home, mine < groups - 1)
    goes_down = jnp.logical_and(mine <= home, mine > 0)

    def pass_on(j):
        @pl.when(goes_up)
        def _():
            relay(j, True).start()

        @pl.when(goes_down)
        def _():
            relay(j, False).start()

    for k in range(1, groups):
        spread(0, k).start()
    for z in range(nz):
        for h in range(ratio):
            @pl.when(ratio * mine + h != me)
            def _():
                collect(z, h).start()

            @pl.when(ratio * mine + h == me)
            def _():
                colv[z, me] = vy_ref[z, :, h * width:(h + 1) * width]
    for c in range(1, len(parts)):
        for k in range(1, groups):
            spread(c, k).start()
    held[mine] = vx_ref[...]

    lane = lax.broadcasted_iota(jnp.int32, (rows, LANES), 1)
    for z in range(nz):
        shift = jnp.transpose(jnp.broadcast_to(sx_ref[z:z + 1, :] + REACH, (LANES, rows)))
        shift_of[z] = shift
        place_of[z] = (lane - shift) & (LANES - 1)

    top = nx // 2
    row = lax.broadcasted_iota(jnp.int32, (2 * ns, top), 0)
    index = jnp.full((2 * ns, top), sc_ref[0], jnp.int32)
    for s in range(1, ns):
        index = jnp.where(row % ns == s, sc_ref[s], index)
    rate = jnp.exp2((3 - index).astype(jnp.float32))
    rate = jnp.where(row < ns, 0.5 * rate, rate)
    relative = lax.broadcasted_iota(jnp.int32, (2 * ns, top), 1).astype(jnp.float32) / top
    damping = jnp.exp(-rate * relative * relative)
    tables.wait()
    g = jnp.dot(damping, cos_ref[...], precision=lax.Precision.HIGHEST, preferred_element_type=jnp.float32)
    last = jnp.exp(-rate[:, 0:1]) / nx
    odd = lax.broadcasted_iota(jnp.int32, (2 * ns, nx), 1) % 2
    g = g + jnp.where(odd == 1, -last, last)
    line[0:ns, :] = pltpu.roll(g, nx - (REACH + 2), 1)[0:ns]
    line[ns:, :] = pltpu.roll(g, REACH + 2, 1)[ns:]

    def circulant(t):
        for r in range(0, LANES, 64):
            wide = jnp.broadcast_to(line[pl.ds(t, 1), :], (64, nx))
            high, low = halves(pltpu.roll(wide, r, 1, stride=1, stride_axis=0))
            for e in range(0, BLOCK, LANES):
                at = slice(r + e, r + e + 64)
                th[t, at, e:], tl[t, at, e:] = high[:, :nx - e], low[:, :nx - e]
                if e:
                    th[t, at, :e], tl[t, at, :e] = high[:, nx - e:], low[:, nx - e:]

    circulant(0)

    def weigh_rows(c):
        z, first_row, n = parts[c]
        for k in range(1, groups):
            spread(c, k).wait_recv()

        @pl.loop(0, n // 8, unroll=2)
        def _(i):
            at = pl.ds(pl.multiple_of(first_row + i * 8, 8), 8)
            f = jnp.concatenate([held[g, z, at, :] for g in range(groups)], axis=1)
            for m, w in enumerate(spline_weights(f)):
                wx[z, m, at, :] = pltpu.roll(w, m % 3, 1) if m % 3 else w

    def remesh_eight(z, at, q):
        one, two = pltpu.roll(q, 1, 1), pltpu.roll(q, 2, 1)
        near = q * wx[z, 0, at, :] + one * wx[z, 1, at, :] + two * wx[z, 2, at, :]
        far = q * wx[z, 3, at, :] + one * wx[z, 4, at, :] + two * wx[z, 5, at, :]
        total = near + pltpu.roll(far, 3, 1)
        place, shift = place_of[z, at, :], shift_of[z, at, :]
        stays = lax.broadcasted_iota(jnp.int32, shift.shape, 1) >= shift
        moved = [
            jnp.take_along_axis(total[:, v:v + LANES], place, axis=1) for v in range(0, nx, LANES)
        ]
        return jnp.concatenate(
            [jnp.where(stays, moved[v], moved[v - 1]) for v in range(nx // LANES)], axis=1
        )

    def remesh_rows(z, first_row, n, read):
        @pl.loop(0, n // STEP, unroll=2)
        def _(i):
            r = pl.multiple_of(first_row + i * STEP, STEP)
            both = [
                remesh_eight(z, pl.ds(pl.multiple_of(r + e, 8), 8), read(pl.ds(pl.multiple_of(r + e, 8), 8)))
                for e in (0, 8)
            ]
            at = pl.ds(r, STEP)
            part_hi[at, :], part_lo[at, :] = halves(jnp.concatenate(both, axis=0))

    def forward(s, c, k):
        z, r, n = parts[c]
        dest = lax.rem(me + k, peers)
        return pltpu.make_async_remote_copy(
            src_ref=ext.at[s, z, dest, pl.ds(r, n), :], dst_ref=cols.at[s, z, me, pl.ds(r, n), :],
            send_sem=send1.at[s, c, k - 1], recv_sem=recv1.at[s, c, k - 1],
            device_id={"space": dest}, device_id_type=MESH,
        )

    def backward(s, z, k):
        dest = lax.rem(me + k, peers)
        return pltpu.make_async_remote_copy(
            src_ref=turned.at[s, dest, z], dst_ref=back.at[s, me, z],
            send_sem=send2.at[s, z, k - 1], recv_sem=recv2.at[s, z, k - 1],
            device_id={"space": dest}, device_id_type=MESH,
        )

    per = BLOCK // width

    def first_sweep(s, c):
        z, r, n = parts[c]
        remesh_rows(z, r, n, lambda at: q_ref[s, z, at, :])

        def store(b, total):
            for h in range(per):
                ext[s, z, b * per + h, r:r + n, :] = total[:, h * width:(h + 1) * width]

        diffuse_rows(part_hi, part_lo, th, tl, s, r, n, store)
        for k in range(1, peers):
            forward(s, c, k).start()
        cols[s, z, me, r:r + n, :] = ext[s, z, me, r:r + n, :]

    def await_relay(j):
        @pl.when(mine != home)
        def _():
            relay(j, True).wait_recv()
            pass_on(j)

    def launch(z):
        @pl.when(mine == home)
        def _():
            for k in range(1, peers):
                collected(z, k).wait_recv()

            @pl.loop(z * (peers // 2), (z + 1) * (peers // 2))
            def _(j):
                pass_on(j)

    count = nz * peers // 2
    for c in range(len(parts)):
        weigh_rows(c)

        @pl.loop(0, ns)
        def _(s):
            if parts[c][1] == 0:
                load(s, parts[c][0]).wait()
            first_sweep(s, c)
            if c == 0:
                circulant(s + 1)
            if c == len(parts) - 1:
                await_relay(s)

        for z in range(nz):
            if c == (1, 1)[z]:
                launch(z)

    reach = 24
    part = 64

    def weigh_columns(z):
        @pl.loop(0, ny // part)
        def _(i):
            y = i * part
            before = lax.rem(y - 8 + ny, ny)
            f = jnp.concatenate(
                [
                    colv[z, before // rows, pl.ds(pl.multiple_of(before % rows, 8), 8), :],
                    colv[z, y // rows, pl.ds(pl.multiple_of(y % rows, part), part), :],
                ],
                axis=0,
            )
            for m, w in enumerate(spline_weights(f)):
                w = pltpu.roll(w, m % 3, 0) if m % 3 else w
                wy[z, m, pl.ds(pl.multiple_of(reach + y, 8), part), :] = w[8:]

        for m in range(6):
            wy[z, m, 0:reach, :] = wy[z, m, ny:ny + reach, :]

    weigh_columns(0)

    @pl.loop(ns, count)
    def _(j):
        await_relay(j)

        @pl.when(j < 2 * ns - 1)
        def _():
            circulant(j + 1)

    for t in range(count + 1, 2 * ns):
        circulant(t)
    for z in range(1, nz):
        weigh_columns(z)

    @pl.loop(0, ns)
    def _(s):
        for c in range(len(parts)):
            for k in range(1, peers):
                forward(s, c, k).wait_recv()

        @pl.loop(0, ny // part)
        def _(i):
            y = i * part
            before = lax.rem(y - reach + ny, ny)
            shift = sy_ref[...] + REACH
            for z in range(nz):
                q = jnp.concatenate(
                    [
                        cols[s, z, before // rows, pl.ds(pl.multiple_of(before % rows, 8), reach), :],
                        cols[s, z, y // rows, pl.ds(pl.multiple_of(y % rows, part), part), :],
                    ],
                    axis=0,
                )
                at = pl.ds(pl.multiple_of(y, part), reach + part)
                one, two = pltpu.roll(q, 1, 0), pltpu.roll(q, 2, 0)
                near = q * wy[z, 0, at, :] + one * wy[z, 1, at, :] + two * wy[z, 2, at, :]
                far = q * wy[z, 3, at, :] + one * wy[z, 4, at, :] + two * wy[z, 5, at, :]
                u = near + pltpu.roll(far, 3, 0)
                for bit in (1, 2, 4, 8, 16):
                    u = jnp.where((shift & bit) != 0, pltpu.roll(u, bit, 0), u)
                put = pl.ds(pl.multiple_of(y, part), part)
                lanes = slice(z * width, (z + 1) * width)
                col_hi[put, lanes], col_lo[put, lanes] = halves(u[reach:])

        for a in range(by):
            total = jnp.zeros((BLOCK, nz * width), jnp.float32)
            for b in range(by):
                d = ((b - a) % by) * BLOCK
                high, low = th[ns + s, :, d:d + BLOCK], tl[ns + s, :, d:d + BLOCK]
                left = col_hi[b * BLOCK:(b + 1) * BLOCK, :]
                rest = col_lo[b * BLOCK:(b + 1) * BLOCK, :]
                total = total + (dot32(high, left) + (dot32(low, left) + dot32(high, rest)))
            for h in range(BLOCK // rows):
                for z in range(nz):
                    turned[s, a * (BLOCK // rows) + h, z] = total[
                        h * rows:(h + 1) * rows, z * width:(z + 1) * width
                    ]
        for z in range(nz):
            for k in range(1, peers):
                backward(s, z, k).start()
        back[s, me] = turned[s, me]

    @pl.loop(0, ns)
    def _(s):
        for z in range(nz):
            for k in range(1, peers):
                backward(s, z, k).wait_recv()
            remesh_rows(
                z, 0, rows,
                lambda at: jnp.concatenate([back[s, p, z, at, :] for p in range(peers)], axis=1),
            )

            def store(b, total):
                out_ref[s, z, :, b * BLOCK:(b + 1) * BLOCK] = total

            @pl.when(s < ns - 1 if z == nz - 1 else s < ns)
            def _():
                diffuse_rows(part_hi, part_lo, th, tl, s, 0, rows, store)

    @pl.loop(0, ns)
    def _(s):
        for k in range(1, peers):
            for c in range(len(parts)):
                forward(s, c, k).wait_send()
            for z in range(nz):
                backward(s, z, k).wait_send()

    for c in range(len(parts)):
        for k in range(1, groups):
            spread(c, k).wait_send()
    for z in range(nz):
        for h in range(ratio):
            @pl.when(ratio * mine + h != me)
            def _():
                collect(z, h).wait_send()

    @pl.loop(0, count)
    def _(j):
        @pl.when(goes_up)
        def _():
            relay(j, True).wait_send()

        @pl.when(goes_down)
        def _():
            relay(j, False).wait_send()


def finish_kernel(held_ref, th, tl, part_hi, part_lo, out_ref, lines, sem, sem_last):
    ns, nz, rows, nx = held_ref.shape
    copies = [
        pltpu.make_async_copy(held_ref.at[s, z], out_ref.at[s, z], sem.at[s, z])
        for s in range(ns) for z in range(nz) if s < ns - 1 or z < nz - 1
    ]
    for copy in copies:
        copy.start()

    def store(b, total):
        lines[b] = total
        copies.append(
            pltpu.make_async_copy(
                lines.at[b], out_ref.at[ns - 1, nz - 1, :, pl.ds(b * BLOCK, BLOCK)], sem_last.at[b]
            )
        )
        copies[-1].start()

    diffuse_rows(part_hi, part_lo, th, tl, ns - 1, 0, rows, store)
    for copy in copies:
        copy.wait()


def transport_on_device(peers, groups, scalars, velocity_x, velocity_y, shift_x, shift_y, schmidt):
    ns, nz, rows, nx = scalars.shape
    ny, width = rows * peers, nx // peers
    f32, bf16, i32 = jnp.float32, jnp.bfloat16, jnp.int32
    vmem = pl.BlockSpec(memory_space=pltpu.VMEM)
    smem = pl.BlockSpec(memory_space=pltpu.SMEM)
    anywhere = pl.BlockSpec(memory_space=pl.ANY)
    count = nz * peers // 2
    dma = pltpu.SemaphoreType.DMA
    result = pl.pallas_call(
        functools.partial(transport_kernel, peers, groups),
        out_shape=[
            pltpu.VMEM(scalars.shape, f32),
            pltpu.VMEM((2 * ns, BLOCK, nx), bf16),
            pltpu.VMEM((2 * ns, BLOCK, nx), bf16),
            pltpu.VMEM((rows, nx), bf16),
            pltpu.VMEM((rows, nx), bf16),
        ],
        in_specs=[anywhere, vmem, vmem, vmem, vmem, smem, anywhere],
        out_specs=[vmem] * 5,
        scratch_shapes=[
            pltpu.VMEM(scalars.shape, f32),
            pltpu.VMEM((nx // 2, nx), f32),
            pltpu.VMEM((2 * ns, nx), f32),
            pltpu.VMEM((nz, rows, LANES), i32),
            pltpu.VMEM((nz, rows, LANES), i32),
            pltpu.VMEM((nz, 6, rows, nx), f32),
            pltpu.VMEM((nz, 6, ny + 24, width), f32),
            pltpu.VMEM((ns, nz, peers, rows, width), f32),
            pltpu.VMEM((ns, nz, peers, rows, width), f32),
            pltpu.VMEM((ny, nz * width), bf16),
            pltpu.VMEM((ny, nz * width), bf16),
            pltpu.VMEM((ns, peers, nz, rows, width), f32),
            pltpu.VMEM((ns, peers, nz, rows, width), f32),
            pltpu.VMEM((groups,) + velocity_x.shape, f32),
            pltpu.VMEM((nz, peers, rows, width), f32),
            dma((ns, nz)),
            dma,
            dma((3, groups - 1)),
            dma((3, groups - 1)),
            dma((nz, peers // groups)),
            dma((nz, peers)),
            dma((count,)),
            dma((count,)),
            dma((count,)),
            dma((ns, 3, peers - 1)),
            dma((ns, 3, peers - 1)),
            dma((ns, nz, peers - 1)),
            dma((ns, nz, peers - 1)),
        ],
        compiler_params=pltpu.CompilerParams(
            collective_id=0, has_side_effects=True, vmem_limit_bytes=42 * 2**20
        ),
    )(
        scalars, velocity_x, velocity_y, shift_x, shift_y[None, :], schmidt,
        jnp.asarray(cosine_table(nx)),
    )
    result = [pltpu.with_memory_space_constraint(r, pltpu.VMEM) for r in result]
    return pl.pallas_call(
        finish_kernel,
        out_shape=jax.ShapeDtypeStruct(scalars.shape, f32),
        in_specs=[vmem] * 5,
        out_specs=anywhere,
        scratch_shapes=[pltpu.VMEM((nx // BLOCK, rows, BLOCK), f32), dma((ns, nz)), dma((nx // BLOCK,))],
        compiler_params=pltpu.CompilerParams(vmem_limit_bytes=6 * 2**20),
    )(*result)


def transport(peers, groups, scalars, *others):
    ns, nz, rows, nx = scalars.shape
    fits = (
        peers % groups == 0 and peers % 2 == 0 and nz == 2 and rows == LANES and nx == rows * peers == NY
        and ns <= nz * peers // 2 and others[0].shape[2] == nx // groups and nx % BLOCK == 0
    )
    if not fits:
        return on_device(scalars, *others)
    return transport_on_device(peers, groups, scalars, *others)


def solution(mesh):
    peers = mesh.shape["space"]
    body = functools.partial(transport, peers, mesh.shape["scalar"])
    return jax.shard_map(
        body,
        mesh=mesh,
        in_specs=(
            P("scalar", None, "space", None),
            P(None, "space", "scalar"),
            P(None, "space", "scalar"),
            P(None, "space"),
            P("space"),
            P("scalar"),
        ),
        out_specs=P("scalar", None, "space", None),
        check_vma=False,
    )
```

```python
import functools
import math

import jax
import jax.numpy as jnp
import numpy as np
from jax import lax
from jax.experimental import pallas as pl
from jax.experimental.pallas import tpu as pltpu
from jax.sharding import PartitionSpec as P

NY = 1024


def spline(distance):
    magnitude = jnp.abs(distance)
    far_part = jnp.maximum(3.0 - magnitude, 0.0)
    middle = jnp.maximum(2.0 - magnitude, 0.0)
    near_part = jnp.maximum(1.0 - magnitude, 0.0)
    return (far_part**5 - 6.0 * middle**5 + 15.0 * near_part**5) / 120.0


def remesh(fields, fraction, shift_line):
    summed = jnp.zeros_like(fields)
    for offset in range(-2, 4):
        weight = spline(offset - fraction)
        summed = summed + jnp.roll(fields * weight, offset, axis=-1)
    line_shift = shift_line[None, :, :, None]
    moved = summed
    for amount in range(-8, 9):
        moved = jnp.where(line_shift == amount, jnp.roll(summed, amount, axis=-1), moved)
    return moved


def remesh_columns(fields, fraction, shift_cols):
    summed = jnp.zeros_like(fields)
    for offset in range(-2, 4):
        weight = spline(offset - fraction)
        summed = summed + jnp.roll(fields * weight[None], offset, axis=2)
    column_shift = shift_cols[None, None, None, :]
    moved = summed
    for amount in range(-8, 9):
        moved = jnp.where(column_shift == amount, jnp.roll(summed, amount, axis=2), moved)
    return moved


def spectral_tables(length):
    midpoint = length // 2
    column = jnp.arange(length, dtype=jnp.int32)
    wavenum = jnp.where(column <= midpoint, column, column - midpoint)
    phases = column[:, None] * wavenum[None, :] % length
    angles = phases.astype(jnp.float32) * (2.0 * math.pi / length)
    forward = jnp.where((column <= midpoint)[None, :], jnp.cos(angles), jnp.sin(angles))
    inverse_weight = jnp.where((wavenum == 0) | (column == midpoint), 1.0, 2.0) / length
    inverse = forward.T * inverse_weight[:, None]
    relative = wavenum.astype(jnp.float32) / midpoint
    return (forward, inverse, relative * relative)


def diffuse(fields, diffusivity, tables):
    forward, inverse, wave_square = tables
    initial = fields.shape
    rows_flat = fields.reshape(-1, initial[-1])
    spectra = jnp.dot(
        rows_flat, forward, precision=lax.Precision.HIGHEST, preferred_element_type=jnp.float32
    )
    damping = jnp.exp(-diffusivity[:, None] * wave_square[None, :])
    spectra = spectra.reshape(initial) * damping[:, None, None, :]
    result = jnp.dot(
        spectra.reshape(-1, initial[-1]),
        inverse,
        precision=lax.Precision.HIGHEST,
        preferred_element_type=jnp.float32,
    )
    return result.reshape(initial)


def diffuse_columns(fields, diffusivity, tables):
    forward, inverse, wave_square = tables
    spectra = jnp.einsum(
        "jk,szjx->szkx",
        forward,
        fields,
        precision=lax.Precision.HIGHEST,
        preferred_element_type=jnp.float32,
    )
    damping = jnp.exp(-diffusivity[:, None] * wave_square[None, :])
    spectra = spectra * damping[:, None, :, None]
    return jnp.einsum(
        "kj,szkx->szjx",
        inverse,
        spectra,
        precision=lax.Precision.HIGHEST,
        preferred_element_type=jnp.float32,
    )


def one_sweep(fields, fraction, shift_line, diffusivity, tables):
    return diffuse(remesh(fields, fraction, shift_line), diffusivity, tables)


def fetch_velocity(velocity_x):
    return lax.all_gather(velocity_x, "scalar", axis=2, tiled=True)


def on_device(scalars, velocity_x, velocity_y, shift_x, shift_y, schmidt):
    diffusivity = jnp.exp2((3 - schmidt).astype(jnp.float32))
    tables_x = spectral_tables(scalars.shape[3])
    tables_y = spectral_tables(NY)
    along_x = fetch_velocity(velocity_x)
    fields = one_sweep(scalars, along_x, shift_x, 0.5 * diffusivity, tables_x)
    along_y = lax.all_gather(velocity_y, "scalar", axis=2, tiled=True)
    fields_cols, velocity_cols = (
        lax.all_to_all(fields, "space", split_axis=3, concat_axis=2, tiled=True),
        lax.all_to_all(along_y[None], "space", split_axis=3, concat_axis=2, tiled=True),
    )
    remeshed = remesh_columns(fields_cols, velocity_cols[0], shift_y)
    returned = diffuse_columns(remeshed, diffusivity, tables_y)
    fields = lax.all_to_all(returned, "space", split_axis=2, concat_axis=3, tiled=True)
    along_x = fetch_velocity(velocity_x)
    return one_sweep(fields, along_x, shift_x, 0.5 * diffusivity, tables_x)


BLOCK = 256
REACH = 8
MESH = pl.DeviceIdType.MESH


def spline_weights(f):
    g = 1.0 - f

    def fifth(v):
        w = v * v
        return w * w * v

    f0, f1, f2 = fifth(f), fifth(1.0 + f), fifth(2.0 + f)
    g0, g1, g2 = fifth(g), fifth(1.0 + g), fifth(2.0 + g)
    c = 1.0 / 120.0
    return (
        g0 * c,
        (g1 - 6.0 * g0) * c,
        (g2 - 6.0 * g1 + 15.0 * g0) * c,
        (f2 - 6.0 * f1 + 15.0 * f0) * c,
        (f1 - 6.0 * f0) * c,
        f0 * c,
    )


STEP = 16
LANES = 128


def cosine_table(length):
    half = length // 2
    k = np.arange(half)
    weight = np.where(k == 0, 1.0, 2.0) / length
    phase = (k[:, None] * np.arange(length)[None, :]) % length
    return (np.cos(phase * (2.0 * np.pi / length)) * weight[:, None]).astype(np.float32)


def halves(v):
    high = v.astype(jnp.bfloat16)
    return high, (v - high.astype(jnp.float32)).astype(jnp.bfloat16)


def dot32(a, b):
    return jnp.dot(a, b, preferred_element_type=jnp.float32)


def diffuse_rows(part_hi, part_lo, th, tl, s, first_row, n, store):
    at = slice(first_row, first_row + n)
    blocks = part_hi.shape[1] // BLOCK
    for b in range(blocks):
        turns = [((b - a) % blocks) * BLOCK for a in range(blocks)]
        high = jnp.concatenate([th[s, :, d:d + BLOCK] for d in turns], axis=0)
        low = jnp.concatenate([tl[s, :, d:d + BLOCK] for d in turns], axis=0)
        left = part_hi[at, :]
        both = dot32(jnp.concatenate([left, part_lo[at, :]], axis=0), high)
        store(b, both[:n] + (dot32(left, low) + both[n:]))


def transport_kernel(
    peers, groups,
    q_hbm, vx_ref, vy_ref, sx_ref, sy_ref, sc_ref, cos_hbm,
    out_ref, th, tl, part_hi, part_lo,
    q_ref, cos_ref, line, shift_of, place_of, wx, wy,
    ext, cols, col_hi, col_lo, turned, back, held, colv,
    sem_q, sem_c, sendx, recvx, sendv, recvv, send_up, send_down, recv_relay,
    send1, recv1, send2, recv2, send3, recv3,
):
    ns, nz, rows, nx = q_ref.shape
    ny = rows * peers
    width = nx // peers
    ratio = peers // groups
    bx, by = nx // BLOCK, ny // BLOCK
    me = lax.axis_index("space")
    mine = lax.axis_index("scalar")
    home = me // ratio
    half = rows // 2
    parts = ((0, 0, half), (0, half, half), (1, 0, rows))

    def load(s, z):
        return pltpu.make_async_copy(q_hbm.at[s, z], q_ref.at[s, z], sem_q.at[s, z])

    tables = pltpu.make_async_copy(cos_hbm, cos_ref, sem_c)
    tables.start()
    for z in range(nz):
        for s in range(ns):
            load(s, z).start()

    barrier = pltpu.get_barrier_semaphore()
    for k in range(1, peers):
        pl.semaphore_signal(barrier, inc=1, device_id={"space": lax.rem(me + k, peers)}, device_id_type=MESH)
    for k in range(1, groups):
        pl.semaphore_signal(barrier, inc=1, device_id={"scalar": lax.rem(mine + k, groups)}, device_id_type=MESH)
    pl.semaphore_wait(barrier, peers + groups - 2)

    def spread(c, k):
        z, r, n = parts[c]
        return pltpu.make_async_remote_copy(
            src_ref=vx_ref.at[z, pl.ds(r, n), :], dst_ref=held.at[mine, z, pl.ds(r, n), :],
            send_sem=sendx.at[c, k - 1], recv_sem=recvx.at[c, k - 1],
            device_id={"scalar": lax.rem(mine + k, groups)}, device_id_type=MESH,
        )

    def collect(z, h):
        dest = ratio * mine + h
        k = lax.rem(dest - me + peers, peers)
        return pltpu.make_async_remote_copy(
            src_ref=vy_ref.at[z, :, pl.ds(h * width, width)], dst_ref=colv.at[z, me],
            send_sem=sendv.at[z, h], recv_sem=recvv.at[z, k],
            device_id={"space": dest}, device_id_type=MESH,
        )

    def collected(z, k):
        return pltpu.make_async_remote_copy(
            src_ref=vy_ref.at[z, :, pl.ds(0, width)], dst_ref=colv.at[z, me],
            send_sem=sendv.at[z, 0], recv_sem=recvv.at[z, k],
            device_id={"space": lax.rem(me + k, peers)}, device_id_type=MESH,
        )

    def relay(j, up):
        z, i = j // (peers // 2), j % (peers // 2)
        block = colv.at[z, pl.ds(2 * i, 2)]
        return pltpu.make_async_remote_copy(
            src_ref=block, dst_ref=block,
            send_sem=(send_up if up else send_down).at[j], recv_sem=recv_relay.at[j],
            device_id={"scalar": lax.rem(mine + (1 if up else groups - 1), groups)}, device_id_type=MESH,
        )

    goes_up = jnp.logical_and(mine >= home, mine < groups - 1)
    goes_down = jnp.logical_and(mine <= home, mine > 0)

    def pass_on(j):
        @pl.when(goes_up)
        def _():
            relay(j, True).start()

        @pl.when(goes_down)
        def _():
            relay(j, False).start()

    for k in range(1, groups):
        spread(0, k).start()
    for z in range(nz):
        for h in range(ratio):
            @pl.when(ratio * mine + h != me)
            def _():
                collect(z, h).start()

            @pl.when(ratio * mine + h == me)
            def _():
                colv[z, me] = vy_ref[z, :, h * width:(h + 1) * width]
    for c in range(1, len(parts)):
        for k in range(1, groups):
            spread(c, k).start()
    held[mine] = vx_ref[...]

    lane = lax.broadcasted_iota(jnp.int32, (rows, LANES), 1)
    for z in range(nz):
        shift = jnp.transpose(jnp.broadcast_to(sx_ref[z:z + 1, :] + REACH, (LANES, rows)))
        shift_of[z] = shift
        place_of[z] = (lane - shift) & (LANES - 1)

    top = nx // 2
    row = lax.broadcasted_iota(jnp.int32, (2 * ns, top), 0)
    index = jnp.full((2 * ns, top), sc_ref[0], jnp.int32)
    for s in range(1, ns):
        index = jnp.where(row % ns == s, sc_ref[s], index)
    rate = jnp.exp2((3 - index).astype(jnp.float32))
    rate = jnp.where(row < ns, 0.5 * rate, rate)
    relative = lax.broadcasted_iota(jnp.int32, (2 * ns, top), 1).astype(jnp.float32) / top
    damping = jnp.exp(-rate * relative * relative)
    tables.wait()
    g = jnp.dot(damping, cos_ref[...], precision=lax.Precision.HIGHEST, preferred_element_type=jnp.float32)
    last = jnp.exp(-rate[:, 0:1]) / nx
    odd = lax.broadcasted_iota(jnp.int32, (2 * ns, nx), 1) % 2
    g = g + jnp.where(odd == 1, -last, last)
    line[0:ns, :] = pltpu.roll(g, nx - (REACH + 2), 1)[0:ns]
    line[ns:, :] = pltpu.roll(g, REACH + 2, 1)[ns:]

    def circulant(t):
        for r in range(0, LANES, 64):
            wide = jnp.broadcast_to(line[pl.ds(t, 1), :], (64, nx))
            high, low = halves(pltpu.roll(wide, r, 1, stride=1, stride_axis=0))
            for e in range(0, BLOCK, LANES):
                at = slice(r + e, r + e + 64)
                th[t, at, e:], tl[t, at, e:] = high[:, :nx - e], low[:, :nx - e]
                if e:
                    th[t, at, :e], tl[t, at, :e] = high[:, nx - e:], low[:, nx - e:]

    circulant(0)

    def weigh_rows(c):
        z, first_row, n = parts[c]
        for k in range(1, groups):
            spread(c, k).wait_recv()

        @pl.loop(0, n // 8, unroll=2)
        def _(i):
            at = pl.ds(pl.multiple_of(first_row + i * 8, 8), 8)
            f = jnp.concatenate([held[g, z, at, :] for g in range(groups)], axis=1)
            for m, w in enumerate(spline_weights(f)):
                wx[z, m, at, :] = pltpu.roll(w, m % 3, 1) if m % 3 else w

    def remesh_eight(z, at, q):
        one, two = pltpu.roll(q, 1, 1), pltpu.roll(q, 2, 1)
        near = q * wx[z, 0, at, :] + one * wx[z, 1, at, :] + two * wx[z, 2, at, :]
        far = q * wx[z, 3, at, :] + one * wx[z, 4, at, :] + two * wx[z, 5, at, :]
        total = near + pltpu.roll(far, 3, 1)
        place, shift = place_of[z, at, :], shift_of[z, at, :]
        stays = lax.broadcasted_iota(jnp.int32, shift.shape, 1) >= shift
        moved = [
            jnp.take_along_axis(total[:, v:v + LANES], place, axis=1) for v in range(0, nx, LANES)
        ]
        return jnp.concatenate(
            [jnp.where(stays, moved[v], moved[v - 1]) for v in range(nx // LANES)], axis=1
        )

    def remesh_rows(z, first_row, n, read):
        @pl.loop(0, n // STEP, unroll=2)
        def _(i):
            r = pl.multiple_of(first_row + i * STEP, STEP)
            both = [
                remesh_eight(z, pl.ds(pl.multiple_of(r + e, 8), 8), read(pl.ds(pl.multiple_of(r + e, 8), 8)))
                for e in (0, 8)
            ]
            at = pl.ds(r, STEP)
            part_hi[at, :], part_lo[at, :] = halves(jnp.concatenate(both, axis=0))

    def forward(s, c, k):
        z, r, n = parts[c]
        dest = lax.rem(me + k, peers)
        return pltpu.make_async_remote_copy(
            src_ref=ext.at[s, z, dest, pl.ds(r, n), :], dst_ref=cols.at[s, z, me, pl.ds(r, n), :],
            send_sem=send1.at[s, c, k - 1], recv_sem=recv1.at[s, c, k - 1],
            device_id={"space": dest}, device_id_type=MESH,
        )

    def backward(s, k):
        dest = lax.rem(me + k, peers)
        return pltpu.make_async_remote_copy(
            src_ref=turned.at[s, dest], dst_ref=back.at[s, me],
            send_sem=send2.at[s, k - 1], recv_sem=recv2.at[s, k - 1],
            device_id={"space": dest}, device_id_type=MESH,
        )

    pieces = ((0, 0, rows), (1, 0, half), (1, half, half))

    def backward_last(c, k):
        z, r, n = pieces[c]
        dest = lax.rem(me + k, peers)
        return pltpu.make_async_remote_copy(
            src_ref=turned.at[ns - 1, dest, z, pl.ds(r, n), :], dst_ref=back.at[ns - 1, me, z, pl.ds(r, n), :],
            send_sem=send3.at[c, k - 1], recv_sem=recv3.at[c, k - 1],
            device_id={"space": dest}, device_id_type=MESH,
        )

    per = BLOCK // width

    def first_sweep(s, c):
        z, r, n = parts[c]
        remesh_rows(z, r, n, lambda at: q_ref[s, z, at, :])

        def store(b, total):
            for h in range(per):
                ext[s, z, b * per + h, r:r + n, :] = total[:, h * width:(h + 1) * width]

        diffuse_rows(part_hi, part_lo, th, tl, s, r, n, store)
        for k in range(1, peers):
            forward(s, c, k).start()
        cols[s, z, me, r:r + n, :] = ext[s, z, me, r:r + n, :]

    def await_relay(j):
        @pl.when(mine != home)
        def _():
            relay(j, True).wait_recv()
            pass_on(j)

    def launch(z):
        @pl.when(mine == home)
        def _():
            for k in range(1, peers):
                collected(z, k).wait_recv()

            @pl.loop(z * (peers // 2), (z + 1) * (peers // 2))
            def _(j):
                pass_on(j)

    count = nz * peers // 2
    for c in range(len(parts)):
        weigh_rows(c)

        @pl.loop(0, ns)
        def _(s):
            if parts[c][1] == 0:
                load(s, parts[c][0]).wait()
            first_sweep(s, c)
            if c == 0:
                circulant(s + 1)
            if c == len(parts) - 1:
                await_relay(s)

        for z in range(nz):
            if c == (1, 1)[z]:
                launch(z)

    reach = 24
    part = 64

    def weigh_columns(z):
        @pl.loop(0, ny // part)
        def _(i):
            y = i * part
            before = lax.rem(y - 8 + ny, ny)
            f = jnp.concatenate(
                [
                    colv[z, before // rows, pl.ds(pl.multiple_of(before % rows, 8), 8), :],
                    colv[z, y // rows, pl.ds(pl.multiple_of(y % rows, part), part), :],
                ],
                axis=0,
            )
            for m, w in enumerate(spline_weights(f)):
                w = pltpu.roll(w, m % 3, 0) if m % 3 else w
                wy[z, m, pl.ds(pl.multiple_of(reach + y, 8), part), :] = w[8:]

        for m in range(6):
            wy[z, m, 0:reach, :] = wy[z, m, ny:ny + reach, :]

    weigh_columns(0)

    @pl.loop(ns, count)
    def _(j):
        await_relay(j)

        @pl.when(j < 2 * ns - 1)
        def _():
            circulant(j + 1)

    for t in range(count + 1, 2 * ns):
        circulant(t)
    for z in range(1, nz):
        weigh_columns(z)

    @pl.loop(0, ns)
    def _(s):
        for c in range(len(parts)):
            for k in range(1, peers):
                forward(s, c, k).wait_recv()

        @pl.loop(0, ny // part)
        def _(i):
            y = i * part
            before = lax.rem(y - reach + ny, ny)
            shift = sy_ref[...] + REACH
            for z in range(nz):
                q = jnp.concatenate(
                    [
                        cols[s, z, before // rows, pl.ds(pl.multiple_of(before % rows, 8), reach), :],
                        cols[s, z, y // rows, pl.ds(pl.multiple_of(y % rows, part), part), :],
                    ],
                    axis=0,
                )
                at = pl.ds(pl.multiple_of(y, part), reach + part)
                one, two = pltpu.roll(q, 1, 0), pltpu.roll(q, 2, 0)
                near = q * wy[z, 0, at, :] + one * wy[z, 1, at, :] + two * wy[z, 2, at, :]
                far = q * wy[z, 3, at, :] + one * wy[z, 4, at, :] + two * wy[z, 5, at, :]
                u = near + pltpu.roll(far, 3, 0)
                for bit in (1, 2, 4, 8, 16):
                    u = jnp.where((shift & bit) != 0, pltpu.roll(u, bit, 0), u)
                put = pl.ds(pl.multiple_of(y, part), part)
                lanes = slice(z * width, (z + 1) * width)
                col_hi[put, lanes], col_lo[put, lanes] = halves(u[reach:])

        for a in range(by):
            total = jnp.zeros((BLOCK, nz * width), jnp.float32)
            for b in range(by):
                d = ((b - a) % by) * BLOCK
                high, low = th[ns + s, :, d:d + BLOCK], tl[ns + s, :, d:d + BLOCK]
                left = col_hi[b * BLOCK:(b + 1) * BLOCK, :]
                rest = col_lo[b * BLOCK:(b + 1) * BLOCK, :]
                total = total + (dot32(high, left) + (dot32(low, left) + dot32(high, rest)))
            for h in range(BLOCK // rows):
                for z in range(nz):
                    turned[s, a * (BLOCK // rows) + h, z] = total[
                        h * rows:(h + 1) * rows, z * width:(z + 1) * width
                    ]
        @pl.when(s < ns - 1)
        def _():
            for k in range(1, peers):
                backward(s, k).start()

        @pl.when(s == ns - 1)
        def _():
            for c in range(len(pieces)):
                for k in range(1, peers):
                    backward_last(c, k).start()

        back[s, me] = turned[s, me]

    def returned(s, z):
        return lambda at: jnp.concatenate([back[s, p, z, at, :] for p in range(peers)], axis=1)

    def finish(s, z):
        def store(b, total):
            out_ref[s, z, :, b * BLOCK:(b + 1) * BLOCK] = total

        diffuse_rows(part_hi, part_lo, th, tl, s, 0, rows, store)

    @pl.loop(0, ns - 1)
    def _(s):
        for k in range(1, peers):
            backward(s, k).wait_recv()
        for z in range(nz):
            remesh_rows(z, 0, rows, returned(s, z))
            finish(s, z)

    for c, (z, r, n) in enumerate(pieces):
        for k in range(1, peers):
            backward_last(c, k).wait_recv()
        remesh_rows(z, r, n, returned(ns - 1, z))
        if c == 0:
            finish(ns - 1, z)

    @pl.loop(0, ns)
    def _(s):
        for k in range(1, peers):
            for c in range(len(parts)):
                forward(s, c, k).wait_send()

    @pl.loop(0, ns - 1)
    def _(s):
        for k in range(1, peers):
            backward(s, k).wait_send()

    for c in range(len(pieces)):
        for k in range(1, peers):
            backward_last(c, k).wait_send()

    for c in range(len(parts)):
        for k in range(1, groups):
            spread(c, k).wait_send()
    for z in range(nz):
        for h in range(ratio):
            @pl.when(ratio * mine + h != me)
            def _():
                collect(z, h).wait_send()

    @pl.loop(0, count)
    def _(j):
        @pl.when(goes_up)
        def _():
            relay(j, True).wait_send()

        @pl.when(goes_down)
        def _():
            relay(j, False).wait_send()


def finish_kernel(held_ref, th, tl, part_hi, part_lo, out_ref, lines, sem, sem_last):
    ns, nz, rows, nx = held_ref.shape
    copies = [
        pltpu.make_async_copy(held_ref.at[s, z], out_ref.at[s, z], sem.at[s, z])
        for s in range(ns) for z in range(nz) if s < ns - 1 or z < nz - 1
    ]
    for copy in copies:
        copy.start()

    def store(b, total):
        lines[b] = total
        copies.append(
            pltpu.make_async_copy(
                lines.at[b], out_ref.at[ns - 1, nz - 1, :, pl.ds(b * BLOCK, BLOCK)], sem_last.at[b]
            )
        )
        copies[-1].start()

    diffuse_rows(part_hi, part_lo, th, tl, ns - 1, 0, rows, store)
    for copy in copies:
        copy.wait()


def transport_on_device(peers, groups, scalars, velocity_x, velocity_y, shift_x, shift_y, schmidt):
    ns, nz, rows, nx = scalars.shape
    ny, width = rows * peers, nx // peers
    f32, bf16, i32 = jnp.float32, jnp.bfloat16, jnp.int32
    vmem = pl.BlockSpec(memory_space=pltpu.VMEM)
    smem = pl.BlockSpec(memory_space=pltpu.SMEM)
    anywhere = pl.BlockSpec(memory_space=pl.ANY)
    count = nz * peers // 2
    dma = pltpu.SemaphoreType.DMA
    result = pl.pallas_call(
        functools.partial(transport_kernel, peers, groups),
        out_shape=[
            pltpu.VMEM(scalars.shape, f32),
            pltpu.VMEM((2 * ns, BLOCK, nx), bf16),
            pltpu.VMEM((2 * ns, BLOCK, nx), bf16),
            pltpu.VMEM((rows, nx), bf16),
            pltpu.VMEM((rows, nx), bf16),
        ],
        in_specs=[anywhere, vmem, vmem, vmem, vmem, smem, anywhere],
        out_specs=[vmem] * 5,
        scratch_shapes=[
            pltpu.VMEM(scalars.shape, f32),
            pltpu.VMEM((nx // 2, nx), f32),
            pltpu.VMEM((2 * ns, nx), f32),
            pltpu.VMEM((nz, rows, LANES), i32),
            pltpu.VMEM((nz, rows, LANES), i32),
            pltpu.VMEM((nz, 6, rows, nx), f32),
            pltpu.VMEM((nz, 6, ny + 24, width), f32),
            pltpu.VMEM((ns, nz, peers, rows, width), f32),
            pltpu.VMEM((ns, nz, peers, rows, width), f32),
            pltpu.VMEM((ny, nz * width), bf16),
            pltpu.VMEM((ny, nz * width), bf16),
            pltpu.VMEM((ns, peers, nz, rows, width), f32),
            pltpu.VMEM((ns, peers, nz, rows, width), f32),
            pltpu.VMEM((groups,) + velocity_x.shape, f32),
            pltpu.VMEM((nz, peers, rows, width), f32),
            dma((ns, nz)),
            dma,
            dma((3, groups - 1)),
            dma((3, groups - 1)),
            dma((nz, peers // groups)),
            dma((nz, peers)),
            dma((count,)),
            dma((count,)),
            dma((count,)),
            dma((ns, 3, peers - 1)),
            dma((ns, 3, peers - 1)),
            dma((ns - 1, peers - 1)),
            dma((ns - 1, peers - 1)),
            dma((3, peers - 1)),
            dma((3, peers - 1)),
        ],
        compiler_params=pltpu.CompilerParams(
            collective_id=0, has_side_effects=True, vmem_limit_bytes=42 * 2**20
        ),
    )(
        scalars, velocity_x, velocity_y, shift_x, shift_y[None, :], schmidt,
        jnp.asarray(cosine_table(nx)),
    )
    result = [pltpu.with_memory_space_constraint(r, pltpu.VMEM) for r in result]
    return pl.pallas_call(
        finish_kernel,
        out_shape=jax.ShapeDtypeStruct(scalars.shape, f32),
        in_specs=[vmem] * 5,
        out_specs=anywhere,
        scratch_shapes=[pltpu.VMEM((nx // BLOCK, rows, BLOCK), f32), dma((ns, nz)), dma((nx // BLOCK,))],
        compiler_params=pltpu.CompilerParams(vmem_limit_bytes=6 * 2**20),
    )(*result)


def transport(peers, groups, scalars, *others):
    ns, nz, rows, nx = scalars.shape
    fits = (
        peers % groups == 0 and peers % 2 == 0 and nz == 2 and rows == LANES and nx == rows * peers == NY
        and ns <= nz * peers // 2 and others[0].shape[2] == nx // groups and nx % BLOCK == 0
    )
    if not fits:
        return on_device(scalars, *others)
    return transport_on_device(peers, groups, scalars, *others)


def solution(mesh):
    peers = mesh.shape["space"]
    body = functools.partial(transport, peers, mesh.shape["scalar"])
    return jax.shard_map(
        body,
        mesh=mesh,
        in_specs=(
            P("scalar", None, "space", None),
            P(None, "space", "scalar"),
            P(None, "space", "scalar"),
            P(None, "space"),
            P("space"),
            P("scalar"),
        ),
        out_specs=P("scalar", None, "space", None),
        check_vma=False,
    )
```

```python
import functools
import math

import jax
import jax.numpy as jnp
import numpy as np
from jax import lax
from jax.experimental import pallas as pl
from jax.experimental.pallas import tpu as pltpu
from jax.sharding import PartitionSpec as P

NY = 1024


def spline(distance):
    magnitude = jnp.abs(distance)
    far_part = jnp.maximum(3.0 - magnitude, 0.0)
    middle = jnp.maximum(2.0 - magnitude, 0.0)
    near_part = jnp.maximum(1.0 - magnitude, 0.0)
    return (far_part**5 - 6.0 * middle**5 + 15.0 * near_part**5) / 120.0


def remesh(fields, fraction, shift_line):
    summed = jnp.zeros_like(fields)
    for offset in range(-2, 4):
        weight = spline(offset - fraction)
        summed = summed + jnp.roll(fields * weight, offset, axis=-1)
    line_shift = shift_line[None, :, :, None]
    moved = summed
    for amount in range(-8, 9):
        moved = jnp.where(line_shift == amount, jnp.roll(summed, amount, axis=-1), moved)
    return moved


def remesh_columns(fields, fraction, shift_cols):
    summed = jnp.zeros_like(fields)
    for offset in range(-2, 4):
        weight = spline(offset - fraction)
        summed = summed + jnp.roll(fields * weight[None], offset, axis=2)
    column_shift = shift_cols[None, None, None, :]
    moved = summed
    for amount in range(-8, 9):
        moved = jnp.where(column_shift == amount, jnp.roll(summed, amount, axis=2), moved)
    return moved


def spectral_tables(length):
    midpoint = length // 2
    column = jnp.arange(length, dtype=jnp.int32)
    wavenum = jnp.where(column <= midpoint, column, column - midpoint)
    phases = column[:, None] * wavenum[None, :] % length
    angles = phases.astype(jnp.float32) * (2.0 * math.pi / length)
    forward = jnp.where((column <= midpoint)[None, :], jnp.cos(angles), jnp.sin(angles))
    inverse_weight = jnp.where((wavenum == 0) | (column == midpoint), 1.0, 2.0) / length
    inverse = forward.T * inverse_weight[:, None]
    relative = wavenum.astype(jnp.float32) / midpoint
    return (forward, inverse, relative * relative)


def diffuse(fields, diffusivity, tables):
    forward, inverse, wave_square = tables
    initial = fields.shape
    rows_flat = fields.reshape(-1, initial[-1])
    spectra = jnp.dot(
        rows_flat, forward, precision=lax.Precision.HIGHEST, preferred_element_type=jnp.float32
    )
    damping = jnp.exp(-diffusivity[:, None] * wave_square[None, :])
    spectra = spectra.reshape(initial) * damping[:, None, None, :]
    result = jnp.dot(
        spectra.reshape(-1, initial[-1]),
        inverse,
        precision=lax.Precision.HIGHEST,
        preferred_element_type=jnp.float32,
    )
    return result.reshape(initial)


def diffuse_columns(fields, diffusivity, tables):
    forward, inverse, wave_square = tables
    spectra = jnp.einsum(
        "jk,szjx->szkx",
        forward,
        fields,
        precision=lax.Precision.HIGHEST,
        preferred_element_type=jnp.float32,
    )
    damping = jnp.exp(-diffusivity[:, None] * wave_square[None, :])
    spectra = spectra * damping[:, None, :, None]
    return jnp.einsum(
        "kj,szkx->szjx",
        inverse,
        spectra,
        precision=lax.Precision.HIGHEST,
        preferred_element_type=jnp.float32,
    )


def one_sweep(fields, fraction, shift_line, diffusivity, tables):
    return diffuse(remesh(fields, fraction, shift_line), diffusivity, tables)


def fetch_velocity(velocity_x):
    return lax.all_gather(velocity_x, "scalar", axis=2, tiled=True)


def on_device(scalars, velocity_x, velocity_y, shift_x, shift_y, schmidt):
    diffusivity = jnp.exp2((3 - schmidt).astype(jnp.float32))
    tables_x = spectral_tables(scalars.shape[3])
    tables_y = spectral_tables(NY)
    along_x = fetch_velocity(velocity_x)
    fields = one_sweep(scalars, along_x, shift_x, 0.5 * diffusivity, tables_x)
    along_y = lax.all_gather(velocity_y, "scalar", axis=2, tiled=True)
    fields_cols, velocity_cols = (
        lax.all_to_all(fields, "space", split_axis=3, concat_axis=2, tiled=True),
        lax.all_to_all(along_y[None], "space", split_axis=3, concat_axis=2, tiled=True),
    )
    remeshed = remesh_columns(fields_cols, velocity_cols[0], shift_y)
    returned = diffuse_columns(remeshed, diffusivity, tables_y)
    fields = lax.all_to_all(returned, "space", split_axis=2, concat_axis=3, tiled=True)
    along_x = fetch_velocity(velocity_x)
    return one_sweep(fields, along_x, shift_x, 0.5 * diffusivity, tables_x)


BLOCK = 256
REACH = 8
MESH = pl.DeviceIdType.MESH


def spline_weights(f):
    g = 1.0 - f

    def fifth(v):
        w = v * v
        return w * w * v

    f0, f1, f2 = fifth(f), fifth(1.0 + f), fifth(2.0 + f)
    g0, g1, g2 = fifth(g), fifth(1.0 + g), fifth(2.0 + g)
    c = 1.0 / 120.0
    return (
        g0 * c,
        (g1 - 6.0 * g0) * c,
        (g2 - 6.0 * g1 + 15.0 * g0) * c,
        (f2 - 6.0 * f1 + 15.0 * f0) * c,
        (f1 - 6.0 * f0) * c,
        f0 * c,
    )


STEP = 16
LANES = 128


def cosine_table(length):
    half = length // 2
    k = np.arange(half)
    weight = np.where(k == 0, 1.0, 2.0) / length
    phase = (k[:, None] * np.arange(length)[None, :]) % length
    return (np.cos(phase * (2.0 * np.pi / length)) * weight[:, None]).astype(np.float32)


def halves(v):
    high = v.astype(jnp.bfloat16)
    return high, (v - high.astype(jnp.float32)).astype(jnp.bfloat16)


def dot32(a, b):
    return jnp.dot(a, b, preferred_element_type=jnp.float32)


def diffuse_rows(part_hi, part_lo, th, tl, s, first_row, n, store):
    at = slice(first_row, first_row + n)
    blocks = part_hi.shape[1] // BLOCK
    for b in range(blocks):
        turns = [((b - a) % blocks) * BLOCK for a in range(blocks)]
        high = jnp.concatenate([th[s, :, d:d + BLOCK] for d in turns], axis=0)
        low = jnp.concatenate([tl[s, :, d:d + BLOCK] for d in turns], axis=0)
        left = part_hi[at, :]
        both = dot32(jnp.concatenate([left, part_lo[at, :]], axis=0), high)
        store(b, both[:n] + (dot32(left, low) + both[n:]))


def transport_kernel(
    peers, groups,
    q_hbm, vx_ref, vy_ref, sx_ref, sy_ref, sc_ref, cos_hbm,
    out_ref, th, tl, part_hi, part_lo,
    q_ref, cos_ref, line, shift_of, place_of, wx, wy,
    ext, cols, col_hi, col_lo, turned, back, held, colv,
    sem_q, sem_c, sendx, recvx, sendv, recvv, send_up, send_down, recv_relay,
    send1, recv1, send2, recv2, send3, recv3,
):
    ns, nz, rows, nx = q_ref.shape
    ny = rows * peers
    width = nx // peers
    ratio = peers // groups
    bx, by = nx // BLOCK, ny // BLOCK
    me = lax.axis_index("space")
    mine = lax.axis_index("scalar")
    home = me // ratio
    half = rows // 2
    parts = ((0, 0, half), (0, half, half), (1, 0, rows))

    def load(s, z):
        return pltpu.make_async_copy(q_hbm.at[s, z], q_ref.at[s, z], sem_q.at[s, z])

    tables = pltpu.make_async_copy(cos_hbm, cos_ref, sem_c)
    tables.start()
    for z in range(nz):
        for s in range(ns):
            load(s, z).start()

    barrier = pltpu.get_barrier_semaphore()
    for k in range(1, peers):
        pl.semaphore_signal(barrier, inc=1, device_id={"space": lax.rem(me + k, peers)}, device_id_type=MESH)
    for k in range(1, groups):
        pl.semaphore_signal(barrier, inc=1, device_id={"scalar": lax.rem(mine + k, groups)}, device_id_type=MESH)
    pl.semaphore_wait(barrier, peers + groups - 2)

    def spread(c, k):
        z, r, n = parts[c]
        return pltpu.make_async_remote_copy(
            src_ref=vx_ref.at[z, pl.ds(r, n), :], dst_ref=held.at[mine, z, pl.ds(r, n), :],
            send_sem=sendx.at[c, k - 1], recv_sem=recvx.at[c, k - 1],
            device_id={"scalar": lax.rem(mine + k, groups)}, device_id_type=MESH,
        )

    def collect(z, h):
        dest = ratio * mine + h
        k = lax.rem(dest - me + peers, peers)
        return pltpu.make_async_remote_copy(
            src_ref=vy_ref.at[z, :, pl.ds(h * width, width)], dst_ref=colv.at[z, me],
            send_sem=sendv.at[z, h], recv_sem=recvv.at[z, k],
            device_id={"space": dest}, device_id_type=MESH,
        )

    def collected(z, k):
        return pltpu.make_async_remote_copy(
            src_ref=vy_ref.at[z, :, pl.ds(0, width)], dst_ref=colv.at[z, me],
            send_sem=sendv.at[z, 0], recv_sem=recvv.at[z, k],
            device_id={"space": lax.rem(me + k, peers)}, device_id_type=MESH,
        )

    def relay(j, up):
        z, i = j // (peers // 2), j % (peers // 2)
        block = colv.at[z, pl.ds(2 * i, 2)]
        return pltpu.make_async_remote_copy(
            src_ref=block, dst_ref=block,
            send_sem=(send_up if up else send_down).at[j], recv_sem=recv_relay.at[j],
            device_id={"scalar": lax.rem(mine + (1 if up else groups - 1), groups)}, device_id_type=MESH,
        )

    goes_up = jnp.logical_and(mine >= home, mine < groups - 1)
    goes_down = jnp.logical_and(mine <= home, mine > 0)

    def pass_on(j):
        @pl.when(goes_up)
        def _():
            relay(j, True).start()

        @pl.when(goes_down)
        def _():
            relay(j, False).start()

    for k in reversed(range(1, groups)):
        spread(0, k).start()
    for z in range(nz):
        for h in range(ratio):
            @pl.when(ratio * mine + h != me)
            def _():
                collect(z, h).start()

            @pl.when(ratio * mine + h == me)
            def _():
                colv[z, me] = vy_ref[z, :, h * width:(h + 1) * width]
    for c in range(1, len(parts)):
        for k in range(1, groups):
            spread(c, k).start()
    held[mine] = vx_ref[...]

    lane = lax.broadcasted_iota(jnp.int32, (rows, LANES), 1)
    for z in range(nz):
        shift = jnp.transpose(jnp.broadcast_to(sx_ref[z:z + 1, :] + REACH, (LANES, rows)))
        shift_of[z] = shift
        place_of[z] = (lane - shift) & (LANES - 1)

    top = nx // 2
    row = lax.broadcasted_iota(jnp.int32, (2 * ns, top), 0)
    index = jnp.full((2 * ns, top), sc_ref[0], jnp.int32)
    for s in range(1, ns):
        index = jnp.where(row % ns == s, sc_ref[s], index)
    rate = jnp.exp2((3 - index).astype(jnp.float32))
    rate = jnp.where(row < ns, 0.5 * rate, rate)
    relative = lax.broadcasted_iota(jnp.int32, (2 * ns, top), 1).astype(jnp.float32) / top
    damping = jnp.exp(-rate * relative * relative)
    tables.wait()
    g = jnp.dot(damping, cos_ref[...], precision=lax.Precision.HIGHEST, preferred_element_type=jnp.float32)
    last = jnp.exp(-rate[:, 0:1]) / nx
    odd = lax.broadcasted_iota(jnp.int32, (2 * ns, nx), 1) % 2
    g = g + jnp.where(odd == 1, -last, last)
    line[0:ns, :] = pltpu.roll(g, nx - (REACH + 2), 1)[0:ns]
    line[ns:, :] = pltpu.roll(g, REACH + 2, 1)[ns:]

    def circulant(t):
        for r in range(0, LANES, 64):
            wide = jnp.broadcast_to(line[pl.ds(t, 1), :], (64, nx))
            high, low = halves(pltpu.roll(wide, r, 1, stride=1, stride_axis=0))
            for e in range(0, BLOCK, LANES):
                at = slice(r + e, r + e + 64)
                th[t, at, e:], tl[t, at, e:] = high[:, :nx - e], low[:, :nx - e]
                if e:
                    th[t, at, :e], tl[t, at, :e] = high[:, nx - e:], low[:, nx - e:]

    circulant(0)

    def weigh_rows(c):
        z, first_row, n = parts[c]
        for k in range(1, groups):
            spread(c, k).wait_recv()

        @pl.loop(0, n // 8, unroll=2)
        def _(i):
            at = pl.ds(pl.multiple_of(first_row + i * 8, 8), 8)
            f = jnp.concatenate([held[g, z, at, :] for g in range(groups)], axis=1)
            for m, w in enumerate(spline_weights(f)):
                wx[z, m, at, :] = pltpu.roll(w, m % 3, 1) if m % 3 else w

    def remesh_eight(z, at, q):
        one, two = pltpu.roll(q, 1, 1), pltpu.roll(q, 2, 1)
        near = q * wx[z, 0, at, :] + one * wx[z, 1, at, :] + two * wx[z, 2, at, :]
        far = q * wx[z, 3, at, :] + one * wx[z, 4, at, :] + two * wx[z, 5, at, :]
        total = near + pltpu.roll(far, 3, 1)
        place, shift = place_of[z, at, :], shift_of[z, at, :]
        stays = lax.broadcasted_iota(jnp.int32, shift.shape, 1) >= shift
        moved = [
            jnp.take_along_axis(total[:, v:v + LANES], place, axis=1) for v in range(0, nx, LANES)
        ]
        return jnp.concatenate(
            [jnp.where(stays, moved[v], moved[v - 1]) for v in range(nx // LANES)], axis=1
        )

    def remesh_rows(z, first_row, n, read):
        @pl.loop(0, n // STEP, unroll=2)
        def _(i):
            r = pl.multiple_of(first_row + i * STEP, STEP)
            both = [
                remesh_eight(z, pl.ds(pl.multiple_of(r + e, 8), 8), read(pl.ds(pl.multiple_of(r + e, 8), 8)))
                for e in (0, 8)
            ]
            at = pl.ds(r, STEP)
            part_hi[at, :], part_lo[at, :] = halves(jnp.concatenate(both, axis=0))

    def forward(s, c, k):
        z, r, n = parts[c]
        dest = lax.rem(me + k, peers)
        return pltpu.make_async_remote_copy(
            src_ref=ext.at[s, z, dest, pl.ds(r, n), :], dst_ref=cols.at[s, z, me, pl.ds(r, n), :],
            send_sem=send1.at[s, c, k - 1], recv_sem=recv1.at[s, c, k - 1],
            device_id={"space": dest}, device_id_type=MESH,
        )

    def backward(s, k):
        dest = lax.rem(me + k, peers)
        return pltpu.make_async_remote_copy(
            src_ref=turned.at[s, dest], dst_ref=back.at[s, me],
            send_sem=send2.at[s, k - 1], recv_sem=recv2.at[s, k - 1],
            device_id={"space": dest}, device_id_type=MESH,
        )

    pieces = ((0, 0, rows), (1, 0, half), (1, half, half))

    def backward_last(c, k):
        z, r, n = pieces[c]
        dest = lax.rem(me + k, peers)
        return pltpu.make_async_remote_copy(
            src_ref=turned.at[ns - 1, dest, z, pl.ds(r, n), :], dst_ref=back.at[ns - 1, me, z, pl.ds(r, n), :],
            send_sem=send3.at[c, k - 1], recv_sem=recv3.at[c, k - 1],
            device_id={"space": dest}, device_id_type=MESH,
        )

    per = BLOCK // width

    def first_sweep(s, c):
        z, r, n = parts[c]
        remesh_rows(z, r, n, lambda at: q_ref[s, z, at, :])

        def store(b, total):
            for h in range(per):
                ext[s, z, b * per + h, r:r + n, :] = total[:, h * width:(h + 1) * width]

        diffuse_rows(part_hi, part_lo, th, tl, s, r, n, store)
        for k in range(1, peers):
            forward(s, c, k).start()
        cols[s, z, me, r:r + n, :] = ext[s, z, me, r:r + n, :]

    def await_relay(j):
        @pl.when(mine != home)
        def _():
            relay(j, True).wait_recv()
            pass_on(j)

    def launch(z):
        @pl.when(mine == home)
        def _():
            for k in range(1, peers):
                collected(z, k).wait_recv()

            @pl.loop(z * (peers // 2), (z + 1) * (peers // 2))
            def _(j):
                pass_on(j)

    count = nz * peers // 2
    for c in range(len(parts)):
        weigh_rows(c)

        @pl.loop(0, ns)
        def _(s):
            if parts[c][1] == 0:
                load(s, parts[c][0]).wait()
            first_sweep(s, c)
            if c == 0:
                circulant(s + 1)
            if c == len(parts) - 1:
                await_relay(s)

        for z in range(nz):
            if c == (1, 1)[z]:
                launch(z)

    reach = 24
    part = 64

    def weigh_columns(z):
        @pl.loop(0, ny // part)
        def _(i):
            y = i * part
            before = lax.rem(y - 8 + ny, ny)
            f = jnp.concatenate(
                [
                    colv[z, before // rows, pl.ds(pl.multiple_of(before % rows, 8), 8), :],
                    colv[z, y // rows, pl.ds(pl.multiple_of(y % rows, part), part), :],
                ],
                axis=0,
            )
            for m, w in enumerate(spline_weights(f)):
                w = pltpu.roll(w, m % 3, 0) if m % 3 else w
                wy[z, m, pl.ds(pl.multiple_of(reach + y, 8), part), :] = w[8:]

        for m in range(6):
            wy[z, m, 0:reach, :] = wy[z, m, ny:ny + reach, :]

    weigh_columns(0)

    @pl.loop(ns, count)
    def _(j):
        await_relay(j)

        @pl.when(j < 2 * ns - 1)
        def _():
            circulant(j + 1)

    for t in range(count + 1, 2 * ns):
        circulant(t)
    for z in range(1, nz):
        weigh_columns(z)

    @pl.loop(0, ns)
    def _(s):
        for c in range(len(parts)):
            for k in range(1, peers):
                forward(s, c, k).wait_recv()

        @pl.loop(0, ny // part)
        def _(i):
            y = i * part
            before = lax.rem(y - reach + ny, ny)
            shift = sy_ref[...] + REACH
            for z in range(nz):
                q = jnp.concatenate(
                    [
                        cols[s, z, before // rows, pl.ds(pl.multiple_of(before % rows, 8), reach), :],
                        cols[s, z, y // rows, pl.ds(pl.multiple_of(y % rows, part), part), :],
                    ],
                    axis=0,
                )
                at = pl.ds(pl.multiple_of(y, part), reach + part)
                one, two = pltpu.roll(q, 1, 0), pltpu.roll(q, 2, 0)
                near = q * wy[z, 0, at, :] + one * wy[z, 1, at, :] + two * wy[z, 2, at, :]
                far = q * wy[z, 3, at, :] + one * wy[z, 4, at, :] + two * wy[z, 5, at, :]
                u = near + pltpu.roll(far, 3, 0)
                for bit in (1, 2, 4, 8, 16):
                    u = jnp.where((shift & bit) != 0, pltpu.roll(u, bit, 0), u)
                put = pl.ds(pl.multiple_of(y, part), part)
                lanes = slice(z * width, (z + 1) * width)
                col_hi[put, lanes], col_lo[put, lanes] = halves(u[reach:])

        for a in range(by):
            total = jnp.zeros((BLOCK, nz * width), jnp.float32)
            for b in range(by):
                d = ((b - a) % by) * BLOCK
                high, low = th[ns + s, :, d:d + BLOCK], tl[ns + s, :, d:d + BLOCK]
                left = col_hi[b * BLOCK:(b + 1) * BLOCK, :]
                rest = col_lo[b * BLOCK:(b + 1) * BLOCK, :]
                total = total + (dot32(high, left) + (dot32(low, left) + dot32(high, rest)))
            for h in range(BLOCK // rows):
                for z in range(nz):
                    turned[s, a * (BLOCK // rows) + h, z] = total[
                        h * rows:(h + 1) * rows, z * width:(z + 1) * width
                    ]
        @pl.when(s < ns - 1)
        def _():
            for k in range(1, peers):
                backward(s, k).start()

        @pl.when(s == ns - 1)
        def _():
            for c in range(len(pieces)):
                for k in range(1, peers):
                    backward_last(c, k).start()

        back[s, me] = turned[s, me]

    def returned(s, z):
        return lambda at: jnp.concatenate([back[s, p, z, at, :] for p in range(peers)], axis=1)

    def finish(s, z):
        def store(b, total):
            out_ref[s, z, :, b * BLOCK:(b + 1) * BLOCK] = total

        diffuse_rows(part_hi, part_lo, th, tl, s, 0, rows, store)

    @pl.loop(0, ns - 1)
    def _(s):
        for k in range(1, peers):
            backward(s, k).wait_recv()
        for z in range(nz):
            remesh_rows(z, 0, rows, returned(s, z))
            finish(s, z)

    for c, (z, r, n) in enumerate(pieces):
        for k in range(1, peers):
            backward_last(c, k).wait_recv()
        remesh_rows(z, r, n, returned(ns - 1, z))
        if c == 0:
            finish(ns - 1, z)

    @pl.loop(0, ns)
    def _(s):
        for k in range(1, peers):
            for c in range(len(parts)):
                forward(s, c, k).wait_send()

    @pl.loop(0, ns - 1)
    def _(s):
        for k in range(1, peers):
            backward(s, k).wait_send()

    for c in range(len(pieces)):
        for k in range(1, peers):
            backward_last(c, k).wait_send()

    for c in range(len(parts)):
        for k in range(1, groups):
            spread(c, k).wait_send()
    for z in range(nz):
        for h in range(ratio):
            @pl.when(ratio * mine + h != me)
            def _():
                collect(z, h).wait_send()

    @pl.loop(0, count)
    def _(j):
        @pl.when(goes_up)
        def _():
            relay(j, True).wait_send()

        @pl.when(goes_down)
        def _():
            relay(j, False).wait_send()


def finish_kernel(held_ref, th, tl, part_hi, part_lo, out_ref, lines, sem, sem_last):
    ns, nz, rows, nx = held_ref.shape
    copies = [
        pltpu.make_async_copy(held_ref.at[s, z], out_ref.at[s, z], sem.at[s, z])
        for s in range(ns) for z in range(nz) if s < ns - 1 or z < nz - 1
    ]
    for copy in copies:
        copy.start()

    def store(b, total):
        lines[b] = total
        copies.append(
            pltpu.make_async_copy(
                lines.at[b], out_ref.at[ns - 1, nz - 1, :, pl.ds(b * BLOCK, BLOCK)], sem_last.at[b]
            )
        )
        copies[-1].start()

    diffuse_rows(part_hi, part_lo, th, tl, ns - 1, 0, rows, store)
    for copy in copies:
        copy.wait()


def transport_on_device(peers, groups, scalars, velocity_x, velocity_y, shift_x, shift_y, schmidt):
    ns, nz, rows, nx = scalars.shape
    ny, width = rows * peers, nx // peers
    f32, bf16, i32 = jnp.float32, jnp.bfloat16, jnp.int32
    vmem = pl.BlockSpec(memory_space=pltpu.VMEM)
    smem = pl.BlockSpec(memory_space=pltpu.SMEM)
    anywhere = pl.BlockSpec(memory_space=pl.ANY)
    count = nz * peers // 2
    dma = pltpu.SemaphoreType.DMA
    result = pl.pallas_call(
        functools.partial(transport_kernel, peers, groups),
        out_shape=[
            pltpu.VMEM(scalars.shape, f32),
            pltpu.VMEM((2 * ns, BLOCK, nx), bf16),
            pltpu.VMEM((2 * ns, BLOCK, nx), bf16),
            pltpu.VMEM((rows, nx), bf16),
            pltpu.VMEM((rows, nx), bf16),
        ],
        in_specs=[anywhere, vmem, vmem, vmem, vmem, smem, anywhere],
        out_specs=[vmem] * 5,
        scratch_shapes=[
            pltpu.VMEM(scalars.shape, f32),
            pltpu.VMEM((nx // 2, nx), f32),
            pltpu.VMEM((2 * ns, nx), f32),
            pltpu.VMEM((nz, rows, LANES), i32),
            pltpu.VMEM((nz, rows, LANES), i32),
            pltpu.VMEM((nz, 6, rows, nx), f32),
            pltpu.VMEM((nz, 6, ny + 24, width), f32),
            pltpu.VMEM((ns, nz, peers, rows, width), f32),
            pltpu.VMEM((ns, nz, peers, rows, width), f32),
            pltpu.VMEM((ny, nz * width), bf16),
            pltpu.VMEM((ny, nz * width), bf16),
            pltpu.VMEM((ns, peers, nz, rows, width), f32),
            pltpu.VMEM((ns, peers, nz, rows, width), f32),
            pltpu.VMEM((groups,) + velocity_x.shape, f32),
            pltpu.VMEM((nz, peers, rows, width), f32),
            dma((ns, nz)),
            dma,
            dma((3, groups - 1)),
            dma((3, groups - 1)),
            dma((nz, peers // groups)),
            dma((nz, peers)),
            dma((count,)),
            dma((count,)),
            dma((count,)),
            dma((ns, 3, peers - 1)),
            dma((ns, 3, peers - 1)),
            dma((ns - 1, peers - 1)),
            dma((ns - 1, peers - 1)),
            dma((3, peers - 1)),
            dma((3, peers - 1)),
        ],
        compiler_params=pltpu.CompilerParams(
            collective_id=0, has_side_effects=True, vmem_limit_bytes=42 * 2**20
        ),
    )(
        scalars, velocity_x, velocity_y, shift_x, shift_y[None, :], schmidt,
        jnp.asarray(cosine_table(nx)),
    )
    result = [pltpu.with_memory_space_constraint(r, pltpu.VMEM) for r in result]
    return pl.pallas_call(
        finish_kernel,
        out_shape=jax.ShapeDtypeStruct(scalars.shape, f32),
        in_specs=[vmem] * 5,
        out_specs=anywhere,
        scratch_shapes=[pltpu.VMEM((nx // BLOCK, rows, BLOCK), f32), dma((ns, nz)), dma((nx // BLOCK,))],
        compiler_params=pltpu.CompilerParams(vmem_limit_bytes=6 * 2**20),
    )(*result)


def transport(peers, groups, scalars, *others):
    ns, nz, rows, nx = scalars.shape
    fits = (
        peers % groups == 0 and peers % 2 == 0 and nz == 2 and rows == LANES and nx == rows * peers == NY
        and ns <= nz * peers // 2 and others[0].shape[2] == nx // groups and nx % BLOCK == 0
    )
    if not fits:
        return on_device(scalars, *others)
    return transport_on_device(peers, groups, scalars, *others)


def solution(mesh):
    peers = mesh.shape["space"]
    body = functools.partial(transport, peers, mesh.shape["scalar"])
    return jax.shard_map(
        body,
        mesh=mesh,
        in_specs=(
            P("scalar", None, "space", None),
            P(None, "space", "scalar"),
            P(None, "space", "scalar"),
            P(None, "space"),
            P("space"),
            P("scalar"),
        ),
        out_specs=P("scalar", None, "space", None),
        check_vma=False,
    )
```
